512 devices in a mesh: shot: 32 (over z, y_hi, core), dom: 16 (over y_lo, x).
Axes of the slice: x: 4, y: 8 (y_hi: 2, y_lo: 4; y = y_hi * 4 + y_lo), z: 8, core: 2. Of those that a mesh axis runs over, the one named last changes fastest.
Arguments:
- vel_coef: float32 [32, 256, 64, 128], P('shot', 'dom'), may hold values from 0.06 to 0.32
- wave_now: float32 [32, 256, 64, 128], P('shot', 'dom'), may hold values from -0.9 to 0.9
- wave_prev: float32 [32, 256, 64, 128], P('shot', 'dom'), may hold values from -0.9 to 0.9
- adjoint_now: float32 [32, 256, 64, 128], P('shot', 'dom'), may hold values from -0.9 to 0.9
- adjoint_prev: float32 [32, 256, 64, 128], P('shot', 'dom'), may hold values from -0.9 to 0.9
- residuals: float32 [32, 4, 64, 128], P('shot'), may hold values from -0.9 to 0.9
- aperture_offset: int32 [32], P('shot'), may hold values from 0 to 16, as said below
- block_count: int32 [32], P('shot'), may hold values from 8 to 16, as said below
Outputs:
- gradient: float32 [32, 256, 4, 128], P('shot', 'dom')
The draws below stay inside these ranges and needn't reach their ends.
Inputs may be any that keep to these rules, and one draw needn't show every extreme that they name: `aperture_offset`: a shot's aperture covers the 16 consecutive model blocks from its offset. The first block_count aperture blocks of a shot lie in the model and add to the gradient.
All inputs are finite; a program needn't handle non-finite values.
Results may differ from the reference program's by a relative error of at most 0.0003.
Values sent between devices are 32-bit elements; how exact they have to be, the bound alone decides.
No kernel may reach another device: no remote copies, remote signals or barrier semaphores. Data moves between devices by JAX's collectives and lax.ppermute only.
A program may use at most 64 MiB of HBM per device.

```python
import math
import jax
import jax.numpy as jnp
from jax import lax

AXW = 64
AY = 128
STEPS = 4
AZ = 256
SHOTS = 32
MBLK = 32
AB = 16
BX = 4


def draw_aperture_offset(key, part):
    key = jax.random.fold_in(key, 11)
    first_key, second_key = jax.random.split(key)
    values = jax.random.randint(first_key, (SHOTS,), 0, MBLK - AB + 1, dtype=jnp.int32)
    order = jax.random.permutation(second_key, SHOTS)
    values = values.at[order[0]].set(0)
    values = values.at[order[1]].set(MBLK - AB)
    return values.astype(jnp.int32)


def draw_block_count(key, part):
    key = jax.random.fold_in(key, 23)
    first_key, second_key = jax.random.split(key)
    values = jax.random.randint(first_key, (SHOTS,), AB // 2, AB + 1, dtype=jnp.int32)
    order = jax.random.permutation(second_key, SHOTS)
    values = values.at[order[0]].set(AB)
    values = values.at[order[1]].set(AB // 2)
    return values.astype(jnp.int32)


def level_of(key, dims, cuts, least, largest):
    factor_of = 1.0
    for axis_at, shards_of in cuts:
        steps = jax.random.uniform(jax.random.fold_in(jax.random.fold_in(key, 6), axis_at), (shards_of,), jnp.float32, least / len(cuts), largest / len(cuts))
        factor_of = factor_of * jnp.repeat(jnp.exp(steps), dims[axis_at] // shards_of).reshape((-1,) + (1,) * (len(dims) - 1 - axis_at))
    return factor_of


def centred(own_key, dims, width, limit, shards=(), held_as=jnp.bfloat16):
    drawn = jax.random.normal(own_key, dims, jnp.float32) * width
    if len(shards) > 0:
        drawn = level_of(own_key, dims, shards, -0.22, 0.18) * drawn
    return jnp.clip(drawn, min=-limit, max=limit).astype(held_as)


def setup_inputs(seed: int = 0) -> dict:
    splits = jax.random.split(jax.random.key(seed), 9)
    return {
        "vel_coef": jnp.clip(jnp.exp(math.log(0.32) - 1.6739764 * jax.random.uniform(splits[0], (SHOTS, AZ, AXW, AY), jnp.float32) ** level_of(splits[0], (SHOTS, AZ, AXW, AY), ((0, 32), (1, 16)), -0.2, 0.2)), 0.06, 0.32),
        "wave_now": centred(splits[1], (SHOTS, AZ, AXW, AY), 0.15, 0.9, ((0, 32), (1, 16)), jnp.float32),
        "wave_prev": centred(splits[2], (SHOTS, AZ, AXW, AY), 0.15, 0.9, ((0, 32), (1, 16)), jnp.float32),
        "adjoint_now": centred(splits[3], (SHOTS, AZ, AXW, AY), 0.15, 0.9, ((0, 32), (1, 16)), jnp.float32),
        "adjoint_prev": centred(splits[4], (SHOTS, AZ, AXW, AY), 0.15, 0.9, ((0, 32), (1, 16)), jnp.float32),
        "residuals": centred(splits[5], (SHOTS, STEPS, AXW, AY), 0.15, 0.9, ((0, 32),), jnp.float32),
        "aperture_offset": draw_aperture_offset(jax.random.fold_in(splits[8], 71), 0),
        "block_count": draw_block_count(jax.random.fold_in(splits[8], 71), 0),
    }


def laplace(values_in):
    padded = jnp.pad(values_in, 1)
    total = padded[2:, 1:-1, 1:-1] + padded[:-2, 1:-1, 1:-1]
    total = total + padded[1:-1, 2:, 1:-1] + padded[1:-1, :-2, 1:-1]
    total = total + padded[1:-1, 1:-1, 2:] + padded[1:-1, 1:-1, :-2]
    return total - 6.0 * values_in


def reference(vel_coef, wave_now, wave_prev, adjoint_now, adjoint_prev, residuals, aperture_offset, block_count):
    def one_shot(gradient_sum, shot_items):
        coefficient, wavefield, previous, adjoint, adjoint_old, injection, first_block, live_count = shot_items
        laplacians = []
        for step_index in range(STEPS):
            laplacian = laplace(wavefield)
            laplacians.append(laplacian)
            wavefield, previous = 2.0 * wavefield - previous + coefficient * laplacian, wavefield
        adjoints = []
        for step_index in range(STEPS):
            updated = 2.0 * adjoint - adjoint_old + laplace(coefficient * adjoint)
            updated = updated.at[0].add(injection[step_index])
            adjoints.append(updated)
            adjoint, adjoint_old = updated, adjoint
        imaging = laplacians[0] * adjoints[STEPS - 1]
        for step_index in range(1, STEPS):
            imaging = imaging + laplacians[step_index] * adjoints[STEPS - 1 - step_index]
        aperture_grads = imaging.reshape(AZ, AB, BX, AY).transpose(1, 0, 2, 3)
        live_mask = (jnp.arange(AB, dtype=jnp.int32) < live_count).astype(jnp.float32)[:, None, None, None]
        first_row = first_block.astype(jnp.int32)
        existing = lax.dynamic_slice_in_dim(gradient_sum, first_row, AB, 0)
        gradient_sum = lax.dynamic_update_slice_in_dim(gradient_sum, existing + aperture_grads * live_mask, first_row, 0)
        return gradient_sum, None

    start_sum = jnp.zeros((MBLK, AZ, BX, AY), jnp.float32)
    gradient_sum, unused = lax.scan(one_shot, start_sum, (vel_coef, wave_now, wave_prev, adjoint_now, adjoint_prev, residuals, aperture_offset, block_count))
    return gradient_sum
```

```python
import functools

import jax
import jax.numpy as jnp
from jax import lax
from jax.experimental import pallas as pl
from jax.experimental.pallas import tpu as pltpu
from jax.sharding import PartitionSpec as P

PAD = 8


def lateral(ref, z, width, first, last):
    middle = ref[z, PAD : PAD + width, :]
    total = ref[z, PAD - 1 : PAD - 1 + width, :] + ref[z, PAD + 1 : PAD + 1 + width, :]
    size = middle.shape[1]
    left = jnp.where(first, 0.0, pltpu.roll(middle, 1, 1))
    right = jnp.where(last, 0.0, pltpu.roll(middle, size - 1, 1))
    return total + (left + right) - 6.0 * middle, middle


def replay(
    steps, depth, width, size, blocks,
    offset, count, vel, wave, wave_old, adj, adj_old, low, high, residuals,
    own, other,
    p0, p1, v, w0, w1, q, img,
):
    h = steps
    slab = lax.axis_index("dom")
    core = lax.rem(lax.axis_index("shot"), 2)
    column = lax.broadcasted_iota(jnp.int32, (width, size), 1)
    first, last = column == 0, column == size - 1
    rows = slice(PAD, PAD + width)
    edge = jnp.zeros((depth + 2 * h, PAD, size), jnp.float32)
    for ref in (p0, p1, w0, w1):
        ref[:, 0:PAD, :] = edge
        ref[:, PAD + width : 2 * PAD + width, :] = edge
    at = [0, h, 2 * h - 1, 3 * h - 1, 4 * h - 1]
    n = depth
    p0[0:h, rows, :] = low[at[0] : at[0] + h]
    p0[h + n : 2 * h + n, rows, :] = high[at[0] : at[0] + h]
    p0[h : h + n, rows, :] = wave[0]
    p1[1:h, rows, :] = low[at[1] : at[1] + h - 1]
    p1[h + n : 2 * h + n - 1, rows, :] = high[at[1] : at[1] + h - 1]
    p1[h : h + n, rows, :] = wave_old[0]
    v[0:h] = low[at[2] : at[2] + h]
    v[h + n : 2 * h + n] = high[at[2] : at[2] + h]
    v[h : h + n] = vel[0]
    q[1, 0:h] = low[at[3] : at[3] + h]
    q[1, h + n : 2 * h + n] = high[at[3] : at[3] + h]
    q[1, h : h + n] = adj[0]
    q[0, 1:h] = low[at[4] : at[4] + h - 1]
    q[0, h + n : 2 * h + n - 1] = high[at[4] : at[4] + h - 1]
    q[0, h : h + n] = adj_old[0]

    @pl.loop(0, n + 2 * h)
    def _(z):
        w0[z, rows, :] = v[z] * q[1, z]

    ws = (w0, w1)
    for step in range(steps):
        source, target = ws[step % 2], ws[(step + 1) % 2]

        @pl.loop(step + 1, n + 2 * h - step - 1)
        def _(z):
            lap, _ = lateral(source, z, width, first, last)
            lap = lap + (source[z - 1, rows, :] + source[z + 1, rows, :])
            new = 2.0 * q[step + 1, z] - q[step, z] + lap
            q[step + 2, z] = new
            target[z, rows, :] = v[z] * new

        @pl.when(slab == 0)
        def _():
            new = q[step + 2, h] + residuals[0, step]
            q[step + 2, h] = new
            target[h, rows, :] = v[h] * new

    ps = (p0, p1)
    for step in range(steps):
        source, target = ps[step % 2], ps[(step + 1) % 2]
        inner = step < steps - 1

        def lap_of(z):
            lap, middle = lateral(source, z, width, first, last)
            lap = lap + (source[z - 1, rows, :] + source[z + 1, rows, :])
            if inner:
                target[z, rows, :] = 2.0 * middle - target[z, rows, :] + v[z] * lap
            return lap

        if inner:
            for begin, end in ((step + 1, h), (h + n, n + 2 * h - step - 1)):

                @pl.loop(begin, end)
                def _(z):
                    lap_of(z)

        @pl.loop(h, h + n)
        def _(z):
            term = lap_of(z) * q[steps + 1 - step, z]
            if step == 0:
                img[z - h] = term
            else:
                img[z - h] += term

    span = width // blocks
    zero = jnp.zeros((n * span, size), jnp.float32)

    @pl.loop(0, blocks)
    def _(k):
        own[k] = zero
        other[k] = zero

    start, live = offset[0], count[0]
    odd = lax.rem(start + core, 2)
    for j in range(blocks):
        k = lax.div(start + j, 2)
        mine = odd == j % 2
        for ref, take in ((own, mine), (other, jnp.logical_not(mine))):

            @pl.when(jnp.logical_and(take, j < live))
            def _(ref=ref):
                for z in range(n):
                    ref[k, z * span : (z + 1) * span, :] = img[z, j * span : (j + 1) * span, :]


def total(parts, out):
    out[...] = jnp.sum(parts[...], axis=0)


def shards(vel, wave, wave_old, adj, adj_old, residuals, offset, count):
    _, depth, width, size = vel.shape
    steps = residuals.shape[1]
    shots, doms = lax.axis_size("shot"), lax.axis_size("dom")
    blocks = shots // 2
    span = width // blocks
    h = steps

    up = [a[0, depth - m :] for a, m in ((wave, h), (wave_old, h - 1), (vel, h), (adj, h), (adj_old, h - 1))]
    down = [a[0, :m] for a, m in ((wave, h), (wave_old, h - 1), (vel, h), (adj, h), (adj_old, h - 1))]
    forward = [(i, i + 1) for i in range(doms - 1)]
    backward = [(i + 1, i) for i in range(doms - 1)]
    low = lax.ppermute(jnp.concatenate(up), "dom", forward)
    high = lax.ppermute(jnp.concatenate(down), "dom", backward)

    smem = pl.BlockSpec(memory_space=pltpu.SMEM)
    vmem = pl.BlockSpec(memory_space=pltpu.VMEM)
    planes = depth + 2 * h
    padded = pltpu.VMEM((planes, width + 2 * PAD, size), jnp.float32)
    block = jax.ShapeDtypeStruct((blocks, depth * span, size), jnp.float32)
    own, other = pl.pallas_call(
        functools.partial(replay, steps, depth, width, size, blocks),
        out_shape=(block, block),
        in_specs=[smem, smem] + [vmem] * 8,
        out_specs=(vmem, vmem),
        scratch_shapes=[
            padded, padded,
            pltpu.VMEM((planes, width, size), jnp.float32),
            padded, padded,
            pltpu.VMEM((steps + 2, planes, width, size), jnp.float32),
            pltpu.VMEM((depth, width, size), jnp.float32),
        ],
        compiler_params=pltpu.CompilerParams(vmem_limit_bytes=40 * 2**20),
    )(offset, count, vel, wave, wave_old, adj, adj_old, low, high, residuals)

    pair = [(s, s + 1 - 2 * (s % 2)) for s in range(shots)]
    both = own + lax.ppermute(other, "shot", pair)
    groups = [[2 * k + c for k in range(blocks)] for c in range(2)]
    parts = lax.all_to_all(both, "shot", 0, 0, tiled=True, axis_index_groups=groups)
    out = pl.pallas_call(
        total,
        out_shape=jax.ShapeDtypeStruct((depth * span, size), jnp.float32),
        in_specs=[vmem],
        out_specs=vmem,
    )(parts)
    return out.reshape(1, depth, span, size)


def solution(mesh):
    field = P("shot", "dom", None, None)
    placed = (field,) * 5 + (P("shot", None, None, None), P("shot"), P("shot"))
    return jax.shard_map(shards, mesh=mesh, in_specs=placed, out_specs=field, check_vma=False)
```

```python
import functools

import jax
import jax.numpy as jnp
from jax import lax
from jax.experimental import pallas as pl
from jax.experimental.pallas import tpu as pltpu
from jax.sharding import PartitionSpec as P

PAD = 8
CHUNK = 2


class Lateral:
    def __init__(self, width, size):
        row = lax.broadcasted_iota(jnp.int32, (width, size), 0)
        column = lax.broadcasted_iota(jnp.int32, (width, size), 1)
        self.width, self.size = width, size
        self.top, self.bottom = row == 0, row == width - 1
        self.first, self.last = column == 0, column == size - 1

    def along(self, middle):
        left = jnp.where(self.first, 0.0, pltpu.roll(middle, 1, 1))
        right = jnp.where(self.last, 0.0, pltpu.roll(middle, self.size - 1, 1))
        return left + right

    def value(self, middle):
        above = jnp.where(self.top, 0.0, pltpu.roll(middle, 1, 0))
        below = jnp.where(self.bottom, 0.0, pltpu.roll(middle, self.width - 1, 0))
        return (above + below) + self.along(middle) - 6.0 * middle

    def plane(self, ref, z):
        middle = ref[z, PAD : PAD + self.width, :]
        total = ref[z, PAD - 1 : PAD - 1 + self.width, :] + ref[z, PAD + 1 : PAD + 1 + self.width, :]
        return total + self.along(middle) - 6.0 * middle, middle


def edges(steps, depth, vel, wave, wave_old, adj, adj_old, residuals, up, down):
    _, _, width, size = vel.shape
    lateral = Lateral(width, size).value
    source = jnp.where(lax.axis_index("dom") == 0, 1.0, 0.0)
    for out, top in ((down, False), (up, True)):
        at = [depth - 1 - k if top else k for k in range(steps)]
        v = [vel[0, z] for z in at]
        out[2 * steps] = v[0]
        out[2 * steps + 1] = v[1]
        now, old = [wave[0, z] for z in at], [wave_old[0, z] for z in at[:-1]]
        out[0] = now[0]
        for step in range(1, steps):
            new = []
            for k in range(steps - step):
                lap = lateral(now[k]) + now[k + 1]
                if k > 0:
                    lap = lap + now[k - 1]
                new.append(2.0 * now[k] - old[k] + v[k] * lap)
            now, old = new, now
            out[step] = now[0]
        now, old = [adj[0, z] for z in at], [adj_old[0, z] for z in at[:-1]]
        scaled = [c * q for c, q in zip(v, now)]
        out[steps] = scaled[0]
        for step in range(1, steps):
            new = []
            for k in range(steps - step):
                lap = lateral(scaled[k]) + scaled[k + 1]
                if k > 0:
                    lap = lap + scaled[k - 1]
                q = 2.0 * now[k] - old[k] + lap
                if k == 0 and not top:
                    q = q + source * residuals[0, step - 1]
                new.append(q)
            now, old = new, now
            scaled = [c * q for c, q in zip(v, now)]
            out[steps + step] = scaled[0]


def slab(steps, depth, *refs):
    vel, wave, wave_old, adj, adj_old, residuals = refs[:6]
    laps, adjoints, img = refs[6 : 6 + steps], refs[6 + steps : 6 + 2 * steps], refs[6 + 2 * steps]
    ps, ws = refs[7 + 2 * steps : 9 + 2 * steps], refs[9 + 2 * steps : 11 + 2 * steps]
    _, _, width, size = vel.shape
    lateral = Lateral(width, size).plane
    rows = slice(PAD, PAD + width)
    edge = jnp.zeros((depth + 2, PAD, size), jnp.float32)
    blank = jnp.zeros((width, size), jnp.float32)
    for ref in (*ps, *ws):
        ref[:, 0:PAD, :] = edge
        ref[:, PAD + width : 2 * PAD + width, :] = edge
        ref[0, rows, :] = blank
        ref[depth + 1, rows, :] = blank

    @pl.loop(0, depth)
    def _(z):
        ps[0][z + 1, rows, :] = wave[0, z]
        ws[0][z + 1, rows, :] = vel[0, z] * adj[0, z]

    surface = lax.axis_index("dom") == 0
    for step in range(steps):
        source, target = ws[step % 2], ws[(step + 1) % 2]
        now = (lambda z: adj[0, z]) if step == 0 else (lambda z, r=adjoints[step - 1]: r[z])
        old = (
            (lambda z: adj_old[0, z]) if step == 0
            else (lambda z: adj[0, z]) if step == 1
            else (lambda z, r=adjoints[step - 2]: r[z])
        )

        @pl.loop(0, depth, step=CHUNK)
        def _(begin):
            new = []
            for z in [begin + i for i in range(CHUNK)]:
                lap, _ = lateral(source, z + 1)
                lap = lap + (source[z, rows, :] + source[z + 2, rows, :])
                new.append(2.0 * now(z) - old(z) + lap)
            for i, q in enumerate(new):
                z = begin + i
                adjoints[step][z] = q
                if step < steps - 1:
                    target[z + 1, rows, :] = vel[0, z] * q

        @pl.when(surface)
        def _():
            q = adjoints[step][0] + residuals[0, step]
            adjoints[step][0] = q
            if step < steps - 1:
                target[1, rows, :] = vel[0, 0] * q

    for step in range(steps):
        source, target = ps[step % 2], ps[(step + 1) % 2]
        old = (lambda z: wave_old[0, z]) if step == 0 else (lambda z, r=target: r[z + 1, rows, :])

        @pl.loop(0, depth, step=CHUNK)
        def _(begin):
            new = []
            for z in [begin + i for i in range(CHUNK)]:
                lap, middle = lateral(source, z + 1)
                lap = lap + (source[z, rows, :] + source[z + 2, rows, :])
                term = lap * adjoints[steps - 1 - step][z]
                if step > 0:
                    term = term + img[z]
                field = 2.0 * middle - old(z) + vel[0, z] * lap if step < steps - 1 else None
                new.append((lap, term, field))
            for i, (lap, term, field) in enumerate(new):
                z = begin + i
                laps[step][z] = lap
                img[z] = term
                if field is not None:
                    target[z + 1, rows, :] = field


def finish(steps, depth, blocks, *refs):
    offset, count, vel, up, down, low, high = refs[:7]
    laps, adjoints, img = refs[7 : 7 + steps], refs[7 + steps : 7 + 2 * steps], refs[7 + 2 * steps]
    own, other, blocked = refs[8 + 2 * steps :]
    _, _, width, size = vel.shape
    lateral = Lateral(width, size).value
    span = width // blocks

    def store(z, plane):
        for j in range(blocks):
            blocked[j, z * span : (z + 1) * span, :] = plane[j * span : (j + 1) * span, :]

    for z in range(steps, depth - steps):
        store(z, img[z])

    for sent, got, top in ((down, low, False), (up, high, True)):
        at = [depth - 1 - k if top else k for k in range(steps)]
        here = [vel[0, z] for z in at]
        there = [got[2 * steps], got[2 * steps + 1]]

        def march(first, scale_field):
            f = [sent[first + n] for n in range(steps)]
            g = [got[first + n] for n in range(steps)]
            corrections, fields = [], []
            h_now, h_old, t_now, t_old = [], [], [], []
            for step in range(steps):
                if scale_field:
                    hs = [c * x for c, x in zip(here, h_now)]
                    ts = [c * x for c, x in zip(there, t_now)]
                else:
                    hs, ts = h_now, t_now
                laps_here = []
                for k in range(step + 1):
                    lap = g[step] if k == 0 else hs[k - 1]
                    if k == 0 and step > 0:
                        lap = lap + ts[0]
                    if k < len(hs):
                        lap = lap + lateral(hs[k])
                    if k + 1 < len(hs):
                        lap = lap + hs[k + 1]
                    laps_here.append(lap)
                corrections.append(laps_here)
                last = step == steps - 1
                new_h, new_t = [], []
                if scale_field or not last:
                    for k, lap in enumerate(laps_here):
                        x = lap if scale_field else here[k] * lap
                        if k < len(h_now):
                            x = x + 2.0 * h_now[k]
                        if k < len(h_old):
                            x = x - h_old[k]
                        new_h.append(x)
                if not last:
                    for k in range(min(step + 1, steps - 1 - step)):
                        lap = f[step] if k == 0 else ts[k - 1]
                        if k == 0 and step > 0:
                            lap = lap + hs[0]
                        if k < len(ts):
                            lap = lap + lateral(ts[k])
                        if k + 1 < len(ts):
                            lap = lap + ts[k + 1]
                        x = lap if scale_field else there[k] * lap
                        if k < len(t_now):
                            x = x + 2.0 * t_now[k]
                        if k < len(t_old):
                            x = x - t_old[k]
                        new_t.append(x)
                fields.append(new_h)
                h_now, h_old, t_now, t_old = new_h, h_now, new_t, t_now
            return corrections, fields

        more_laps, _ = march(0, False)
        _, more_adjoints = march(steps, True)
        for k, z in enumerate(at):
            total = None
            for n in range(steps):
                a = laps[n][z]
                if k < len(more_laps[n]):
                    a = a + more_laps[n][k]
                b = adjoints[steps - 1 - n][z]
                if k < len(more_adjoints[steps - 1 - n]):
                    b = b + more_adjoints[steps - 1 - n][k]
                total = a * b if total is None else total + a * b
            store(z, total)

    start, live = offset[0], count[0]
    odd = lax.rem(start + lax.axis_index("shot"), 2)
    zero = jnp.zeros((depth * span, size), jnp.float32)
    half = blocks // 2

    @pl.loop(0, half)
    def _(i):
        for ref, j in ((own, 2 * i + odd), (other, 2 * i + 1 - odd)):
            k = lax.div(start + j, 2)
            ref[k] = jnp.where(j < live, blocked[j], 0.0)
            ref[lax.rem(k + half, blocks)] = zero


def shards(vel, wave, wave_old, adj, adj_old, residuals, offset, count):
    _, depth, width, size = vel.shape
    steps = residuals.shape[1]
    shots, doms = lax.axis_size("shot"), lax.axis_size("dom")
    blocks = shots // 2
    span = width // blocks
    f32 = jnp.float32
    smem = pl.BlockSpec(memory_space=pltpu.SMEM)
    vmem = pl.BlockSpec(memory_space=pltpu.VMEM)
    room = pltpu.CompilerParams(vmem_limit_bytes=24 * 2**20)
    message = jax.ShapeDtypeStruct((2 * steps + 2, width, size), f32)
    field = jax.ShapeDtypeStruct((depth, width, size), f32)
    block = jax.ShapeDtypeStruct((blocks, depth * span, size), f32)

    up, down = pl.pallas_call(
        functools.partial(edges, steps, depth),
        out_shape=(message, message),
        in_specs=[vmem] * 6,
        out_specs=(vmem, vmem),
        compiler_params=room,
    )(vel, wave, wave_old, adj, adj_old, residuals)

    low = lax.ppermute(up, "dom", [(i, i + 1) for i in range(doms - 1)])
    high = lax.ppermute(down, "dom", [(i + 1, i) for i in range(doms - 1)])

    padded = pltpu.VMEM((depth + 2, width + 2 * PAD, size), f32)
    inner = pl.pallas_call(
        functools.partial(slab, steps, depth),
        out_shape=(field,) * (2 * steps + 1),
        in_specs=[vmem] * 6,
        out_specs=(vmem,) * (2 * steps + 1),
        scratch_shapes=[padded] * 4,
        cost_estimate=pl.CostEstimate(flops=40_000_000, bytes_accessed=16_000_000, transcendentals=0),
        compiler_params=room,
    )(vel, wave, wave_old, adj, adj_old, residuals)

    own, other = pl.pallas_call(
        functools.partial(finish, steps, depth, blocks),
        out_shape=(block, block),
        in_specs=[smem, smem] + [vmem] * (6 + 2 * steps),
        out_specs=(vmem, vmem),
        scratch_shapes=[pltpu.VMEM((blocks, depth * span, size), f32)],
        compiler_params=room,
    )(offset, count, vel, up, down, low, high, *inner)

    pair = [(s, s + 1 - 2 * (s % 2)) for s in range(shots)]
    both = own + lax.ppermute(other, "shot", pair)
    groups = [[2 * k + c for k in range(blocks)] for c in range(2)]
    parts = lax.all_to_all(both, "shot", 0, 0, tiled=True, axis_index_groups=groups)
    return jnp.sum(parts, axis=0).reshape(1, depth, span, size)


def solution(mesh):
    field = P("shot", "dom", None, None)
    placed = (field,) * 5 + (P("shot", None, None, None), P("shot"), P("shot"))
    return jax.shard_map(shards, mesh=mesh, in_specs=placed, out_specs=field, check_vma=False)
```

```python
import functools

import jax
import jax.numpy as jnp
from jax import lax
from jax.experimental import pallas as pl
from jax.experimental.pallas import tpu as pltpu
from jax.sharding import PartitionSpec as P

CHUNK = 2


class Lateral:
    def __init__(self, width, size):
        row = lax.broadcasted_iota(jnp.int32, (width, size), 0)
        column = lax.broadcasted_iota(jnp.int32, (width, size), 1)
        self.width, self.size = width, size
        self.top, self.bottom = row == 0, row == width - 1
        self.first, self.last = column == 0, column == size - 1

    def __call__(self, middle):
        above = jnp.where(self.top, 0.0, pltpu.roll(middle, 1, 0))
        below = jnp.where(self.bottom, 0.0, pltpu.roll(middle, self.width - 1, 0))
        left = jnp.where(self.first, 0.0, pltpu.roll(middle, 1, 1))
        right = jnp.where(self.last, 0.0, pltpu.roll(middle, self.size - 1, 1))
        return (above + below) + (left + right) - 6.0 * middle


def edges(steps, depth, vel, wave, wave_old, adj, adj_old, residuals, up, down, *scratch):
    _, _, width, size = vel.shape
    lateral = Lateral(width, size)
    fetched, first_residuals, sems, sem = scratch[:5], scratch[5], scratch[6], scratch[7]
    copies = []
    for i, (ref, held) in enumerate(zip((vel, wave, wave_old, adj, adj_old), fetched)):
        for side, begin in enumerate((0, depth - steps)):
            copies.append(pltpu.make_async_copy(ref.at[0, pl.ds(begin, steps)], held.at[side], sems.at[i, side]))
    copies.append(pltpu.make_async_copy(residuals.at[0], first_residuals, sem))
    for copy in copies:
        copy.start()
    for copy in copies:
        copy.wait()
    vel, wave, wave_old, adj, adj_old = fetched
    source = jnp.where(lax.axis_index("dom") == 0, 1.0, 0.0)
    for out, top in ((down, False), (up, True)):
        side = int(top)
        at = [steps - 1 - k if top else k for k in range(steps)]
        v = [vel[side, z] for z in at]
        out[2 * steps] = v[0]
        out[2 * steps + 1] = v[1]
        now, old = [wave[side, z] for z in at], [wave_old[side, z] for z in at[:-1]]
        out[0] = now[0]
        for step in range(1, steps):
            new = []
            for k in range(steps - step):
                lap = lateral(now[k]) + now[k + 1]
                if k > 0:
                    lap = lap + now[k - 1]
                new.append(2.0 * now[k] - old[k] + v[k] * lap)
            now, old = new, now
            out[step] = now[0]
        now, old = [adj[side, z] for z in at], [adj_old[side, z] for z in at[:-1]]
        scaled = [c * q for c, q in zip(v, now)]
        out[steps] = scaled[0]
        for step in range(1, steps):
            new = []
            for k in range(steps - step):
                lap = lateral(scaled[k]) + scaled[k + 1]
                if k > 0:
                    lap = lap + scaled[k - 1]
                q = 2.0 * now[k] - old[k] + lap
                if k == 0 and not top:
                    q = q + source * first_residuals[step - 1]
                new.append(q)
            now, old = new, now
            scaled = [c * q for c, q in zip(v, now)]
            out[steps + step] = scaled[0]


def slab(steps, depth, *refs):
    vel, wave, wave_old, adj, adj_old, residuals = [ref.at[0] for ref in refs[:6]]
    refs = refs[6:]
    laps, adjoints, img = refs[:steps], refs[steps : 2 * steps], refs[2 * steps]
    refs = refs[2 * steps + 1 :]
    ps, ws = refs[:2], refs[2:]
    _, width, size = vel.shape
    lateral = Lateral(width, size)
    blank = jnp.zeros((width, size), jnp.float32)
    for ref in (*ps, *ws):
        ref[0] = blank
        ref[depth + 1] = blank

    @pl.loop(0, depth, step=CHUNK)
    def _(begin):
        for z in [begin + i for i in range(CHUNK)]:
            ps[0][z + 1] = wave[z]
            ws[0][z + 1] = vel[z] * adj[z]

    surface = lax.axis_index("dom") == 0
    fields = (adj_old, adj, *adjoints)
    for step in range(steps):
        source, target = ws[step % 2], ws[(step + 1) % 2]
        old, now, new_field = fields[step : step + 3]

        @pl.loop(0, depth, step=CHUNK)
        def _(begin):
            new = []
            for z in [begin + i for i in range(CHUNK)]:
                lap = lateral(source[z + 1]) + (source[z] + source[z + 2])
                new.append(2.0 * now[z] - old[z] + lap)
            for i, q in enumerate(new):
                new_field[begin + i] = q
            if step < steps - 1:
                scaled = [vel[begin + i] * q for i, q in enumerate(new)]
                for i, w in enumerate(scaled):
                    target[begin + i + 1] = w

        @pl.when(surface)
        def _():
            q = new_field[0] + residuals[step]
            new_field[0] = q
            if step < steps - 1:
                target[1] = vel[0] * q

    for step in range(steps):
        source, target = ps[step % 2], ps[(step + 1) % 2]

        @pl.loop(0, depth, step=CHUNK)
        def _(begin):
            new = []
            for z in [begin + i for i in range(CHUNK)]:
                middle = source[z + 1]
                lap = lateral(middle) + (source[z] + source[z + 2])
                term = lap * adjoints[steps - 1 - step][z]
                if step > 0:
                    term = term + img[z]
                field = None
                if step < steps - 1:
                    old = wave_old[z] if step == 0 else target[z + 1]
                    field = 2.0 * middle - old + vel[z] * lap
                new.append((lap, term, field))
            for i, (lap, term, field) in enumerate(new):
                laps[step][begin + i] = lap
                img[begin + i] = term
                if field is not None:
                    target[begin + i + 1] = field


def finish(steps, depth, blocks, *refs):
    offset, count, vel, up, down, low, high = refs[:7]
    vel = vel.at[0]
    laps, adjoints, img = refs[7 : 7 + steps], refs[7 + steps : 7 + 2 * steps], refs[7 + 2 * steps]
    own, other, blocked = refs[8 + 2 * steps :]
    _, width, size = vel.shape
    lateral = Lateral(width, size)
    span = width // blocks

    def store(z, plane):
        for j in range(blocks):
            blocked[j, z * span : (z + 1) * span, :] = plane[j * span : (j + 1) * span, :]

    for z in range(steps, depth - steps):
        store(z, img[z])

    for sent, got, top in ((down, low, False), (up, high, True)):
        at = [depth - 1 - k if top else k for k in range(steps)]
        here = [vel[z] for z in at]
        there = [got[2 * steps], got[2 * steps + 1]]

        def march(first, scale_field):
            f = [sent[first + n] for n in range(steps)]
            g = [got[first + n] for n in range(steps)]
            corrections, fields = [], []
            h_now, h_old, t_now, t_old = [], [], [], []
            for step in range(steps):
                if scale_field:
                    hs = [c * x for c, x in zip(here, h_now)]
                    ts = [c * x for c, x in zip(there, t_now)]
                else:
                    hs, ts = h_now, t_now
                laps_here = []
                for k in range(step + 1):
                    lap = g[step] if k == 0 else hs[k - 1]
                    if k == 0 and step > 0:
                        lap = lap + ts[0]
                    if k < len(hs):
                        lap = lap + lateral(hs[k])
                    if k + 1 < len(hs):
                        lap = lap + hs[k + 1]
                    laps_here.append(lap)
                corrections.append(laps_here)
                last = step == steps - 1
                new_h, new_t = [], []
                if scale_field or not last:
                    for k, lap in enumerate(laps_here):
                        x = lap if scale_field else here[k] * lap
                        if k < len(h_now):
                            x = x + 2.0 * h_now[k]
                        if k < len(h_old):
                            x = x - h_old[k]
                        new_h.append(x)
                if not last:
                    for k in range(min(step + 1, steps - 1 - step)):
                        lap = f[step] if k == 0 else ts[k - 1]
                        if k == 0 and step > 0:
                            lap = lap + hs[0]
                        if k < len(ts):
                            lap = lap + lateral(ts[k])
                        if k + 1 < len(ts):
                            lap = lap + ts[k + 1]
                        x = lap if scale_field else there[k] * lap
                        if k < len(t_now):
                            x = x + 2.0 * t_now[k]
                        if k < len(t_old):
                            x = x - t_old[k]
                        new_t.append(x)
                fields.append(new_h)
                h_now, h_old, t_now, t_old = new_h, h_now, new_t, t_now
            return corrections, fields

        more_laps, _ = march(0, False)
        _, more_adjoints = march(steps, True)
        for k, z in enumerate(at):
            total = None
            for n in range(steps):
                a = laps[n][z]
                if k < len(more_laps[n]):
                    a = a + more_laps[n][k]
                b = adjoints[steps - 1 - n][z]
                if k < len(more_adjoints[steps - 1 - n]):
                    b = b + more_adjoints[steps - 1 - n][k]
                total = a * b if total is None else total + a * b
            store(z, total)

    start, live = offset[0], count[0]
    odd = lax.rem(start + lax.axis_index("shot"), 2)
    zero = jnp.zeros((depth * span, size), jnp.float32)
    half = blocks // 2

    @pl.loop(0, half)
    def _(i):
        for ref, j in ((own, 2 * i + odd), (other, 2 * i + 1 - odd)):
            k = lax.div(start + j, 2)
            ref[k] = jnp.where(j < live, blocked[j], 0.0)
            ref[lax.rem(k + half, blocks)] = zero


def shards(vel, wave, wave_old, adj, adj_old, residuals, offset, count):
    _, depth, width, size = vel.shape
    steps = residuals.shape[1]
    shots, doms = lax.axis_size("shot"), lax.axis_size("dom")
    blocks = shots // 2
    span = width // blocks
    f32 = jnp.float32
    hbm = pl.BlockSpec(memory_space=pltpu.HBM)
    smem = pl.BlockSpec(memory_space=pltpu.SMEM)
    vmem = pl.BlockSpec(memory_space=pltpu.VMEM)
    room = pltpu.CompilerParams(vmem_limit_bytes=24 * 2**20)
    message = jax.ShapeDtypeStruct((2 * steps + 2, width, size), f32)
    field = jax.ShapeDtypeStruct((depth, width, size), f32)
    block = jax.ShapeDtypeStruct((blocks, depth * span, size), f32)

    up, down = pl.pallas_call(
        functools.partial(edges, steps, depth),
        out_shape=(message, message),
        in_specs=[hbm] * 6,
        out_specs=(vmem, vmem),
        scratch_shapes=[pltpu.VMEM((2, steps, width, size), f32)] * 5
        + [pltpu.VMEM((steps, width, size), f32), pltpu.SemaphoreType.DMA((5, 2)), pltpu.SemaphoreType.DMA],
        compiler_params=pltpu.CompilerParams(vmem_limit_bytes=60 * 2**20),
    )(vel, wave, wave_old, adj, adj_old, residuals)

    low = lax.ppermute(up, "dom", [(i, i + 1) for i in range(doms - 1)])
    high = lax.ppermute(down, "dom", [(i + 1, i) for i in range(doms - 1)])

    inner = pl.pallas_call(
        functools.partial(slab, steps, depth),
        out_shape=(field,) * (2 * steps + 1),
        in_specs=[vmem] * 6,
        out_specs=(vmem,) * (2 * steps + 1),
        scratch_shapes=[pltpu.VMEM((depth + 2, width, size), f32)] * 4,
        cost_estimate=pl.CostEstimate(flops=40_000_000, bytes_accessed=16_000_000, transcendentals=0),
        compiler_params=room,
    )(vel, wave, wave_old, adj, adj_old, residuals)

    own, other = pl.pallas_call(
        functools.partial(finish, steps, depth, blocks),
        out_shape=(block, block),
        in_specs=[smem, smem] + [vmem] * (6 + 2 * steps),
        out_specs=(vmem, vmem),
        scratch_shapes=[pltpu.VMEM((blocks, depth * span, size), f32)],
        compiler_params=room,
    )(offset, count, vel, up, down, low, high, *inner)

    pair = [(s, s + 1 - 2 * (s % 2)) for s in range(shots)]
    both = own + lax.ppermute(other, "shot", pair)
    groups = [[2 * k + c for k in range(blocks)] for c in range(2)]
    parts = lax.all_to_all(both, "shot", 0, 0, tiled=True, axis_index_groups=groups)
    return jnp.sum(parts, axis=0).reshape(1, depth, span, size)


def solution(mesh):
    field = P("shot", "dom", None, None)
    placed = (field,) * 5 + (P("shot", None, None, None), P("shot"), P("shot"))
    return jax.shard_map(shards, mesh=mesh, in_specs=placed, out_specs=field, check_vma=False)
```

```python
import functools

import jax
import jax.numpy as jnp
from jax import lax
from jax.experimental import pallas as pl
from jax.experimental.pallas import tpu as pltpu
from jax.sharding import PartitionSpec as P


class Lateral:
    def __init__(self, width, size):
        row = lax.broadcasted_iota(jnp.int32, (width, size), 0)
        column = lax.broadcasted_iota(jnp.int32, (width, size), 1)
        self.width, self.size = width, size
        self.top, self.bottom = row == 0, row == width - 1
        self.first, self.last = column == 0, column == size - 1

    def __call__(self, middle):
        above = jnp.where(self.top, 0.0, pltpu.roll(middle, 1, 0))
        below = jnp.where(self.bottom, 0.0, pltpu.roll(middle, self.width - 1, 0))
        left = jnp.where(self.first, 0.0, pltpu.roll(middle, 1, 1))
        right = jnp.where(self.last, 0.0, pltpu.roll(middle, self.size - 1, 1))
        return (above + below) + (left + right) - 6.0 * middle


def edges(steps, depth, vel, wave, wave_old, adj, adj_old, up, down, *scratch):
    _, _, width, size = vel.shape
    lateral = Lateral(width, size)
    fetched, sems = scratch[:5], scratch[5]
    copies = []
    for i, (ref, held) in enumerate(zip((vel, wave, wave_old, adj, adj_old), fetched)):
        for side, begin in enumerate((0, depth - steps)):
            copies.append(pltpu.make_async_copy(ref.at[0, pl.ds(begin, steps)], held.at[side], sems.at[i, side]))
    for copy in copies:
        copy.start()
    for copy in copies:
        copy.wait()
    vel, wave, wave_old, adj, adj_old = fetched
    for out, top in ((down, False), (up, True)):
        side = int(top)
        at = [steps - 1 - k if top else k for k in range(steps)]
        v = [vel[side, z] for z in at]
        out[2 * steps] = v[0]
        out[2 * steps + 1] = v[1]
        now, old = [wave[side, z] for z in at], [wave_old[side, z] for z in at[:-1]]
        out[0] = now[0]
        for step in range(1, steps):
            new = []
            for k in range(steps - step):
                lap = lateral(now[k]) + now[k + 1]
                if k > 0:
                    lap = lap + now[k - 1]
                new.append(2.0 * now[k] - old[k] + v[k] * lap)
            now, old = new, now
            out[step] = now[0]
        now, old = [adj[side, z] for z in at], [adj_old[side, z] for z in at[:-1]]
        scaled = [c * q for c, q in zip(v, now)]
        out[steps] = scaled[0]
        for step in range(1, steps):
            new = []
            for k in range(steps - step):
                lap = lateral(scaled[k]) + scaled[k + 1]
                if k > 0:
                    lap = lap + scaled[k - 1]
                new.append(2.0 * now[k] - old[k] + lap)
            now, old = new, now
            scaled = [c * q for c, q in zip(v, now)]
            out[steps + step] = scaled[0]


def slab(steps, depth, *refs):
    vel, wave, wave_old, adj, adj_old, residuals = [ref.at[0] for ref in refs[:6]]
    refs = refs[6:]
    laps, adjoints, img = refs[:steps], refs[steps : 2 * steps], refs[2 * steps]
    refs = refs[2 * steps + 1 :]
    ps, ws = refs[:2], refs[2:]
    _, width, size = vel.shape
    lateral = Lateral(width, size)
    blank = jnp.zeros((width, size), jnp.float32)
    for ref in (*ps, *ws):
        ref[0] = blank
        ref[depth + 1] = blank

    for z in range(depth):
        ps[0][z + 1] = wave[z]
        ws[0][z + 1] = vel[z] * adj[z]

    surface = jnp.where(lax.axis_index("dom") == 0, 1.0, 0.0)
    fields = (adj_old, adj, *adjoints)
    for step in range(steps):
        source, target = ws[step % 2], ws[(step + 1) % 2]
        old, now, new = fields[step : step + 3]
        for z in range(depth):
            lap = lateral(source[z + 1]) + (source[z] + source[z + 2])
            q = 2.0 * now[z] - old[z] + lap
            if z == 0:
                q = q + surface * residuals[step]
            new[z] = q
            if step < steps - 1:
                target[z + 1] = vel[z] * q

    for step in range(steps):
        source, target = ps[step % 2], ps[(step + 1) % 2]
        for z in range(depth):
            middle = source[z + 1]
            lap = lateral(middle) + (source[z] + source[z + 2])
            term = lap * adjoints[steps - 1 - step][z]
            if step > 0:
                term = term + img[z]
            laps[step][z] = lap
            img[z] = term
            if step < steps - 1:
                old = wave_old[z] if step == 0 else target[z + 1]
                target[z + 1] = 2.0 * middle - old + vel[z] * lap


def finish(steps, depth, blocks, *refs):
    offset, count, vel, up, down, low, high = refs[:7]
    vel = vel.at[0]
    laps, adjoints, img = refs[7 : 7 + steps], refs[7 + steps : 7 + 2 * steps], refs[7 + 2 * steps]
    own, other, blocked = refs[8 + 2 * steps :]
    _, width, size = vel.shape
    lateral = Lateral(width, size)
    span = width // blocks

    def store(z, plane):
        for j in range(blocks):
            blocked[j, z * span : (z + 1) * span, :] = plane[j * span : (j + 1) * span, :]

    for z in range(steps, depth - steps):
        store(z, img[z])

    for sent, got, top in ((down, low, False), (up, high, True)):
        at = [depth - 1 - k if top else k for k in range(steps)]
        here = [vel[z] for z in at]
        there = [got[2 * steps], got[2 * steps + 1]]

        def march(first, scale_field):
            f = [sent[first + n] for n in range(steps)]
            g = [got[first + n] for n in range(steps)]
            corrections, fields = [], []
            h_now, h_old, t_now, t_old = [], [], [], []
            for step in range(steps):
                if scale_field:
                    hs = [c * x for c, x in zip(here, h_now)]
                    ts = [c * x for c, x in zip(there, t_now)]
                else:
                    hs, ts = h_now, t_now
                laps_here = []
                for k in range(step + 1):
                    lap = g[step] if k == 0 else hs[k - 1]
                    if k == 0 and step > 0:
                        lap = lap + ts[0]
                    if k < len(hs):
                        lap = lap + lateral(hs[k])
                    if k + 1 < len(hs):
                        lap = lap + hs[k + 1]
                    laps_here.append(lap)
                corrections.append(laps_here)
                last = step == steps - 1
                new_h, new_t = [], []
                if scale_field or not last:
                    for k, lap in enumerate(laps_here):
                        x = lap if scale_field else here[k] * lap
                        if k < len(h_now):
                            x = x + 2.0 * h_now[k]
                        if k < len(h_old):
                            x = x - h_old[k]
                        new_h.append(x)
                if not last:
                    for k in range(min(step + 1, steps - 1 - step)):
                        lap = f[step] if k == 0 else ts[k - 1]
                        if k == 0 and step > 0:
                            lap = lap + hs[0]
                        if k < len(ts):
                            lap = lap + lateral(ts[k])
                        if k + 1 < len(ts):
                            lap = lap + ts[k + 1]
                        x = lap if scale_field else there[k] * lap
                        if k < len(t_now):
                            x = x + 2.0 * t_now[k]
                        if k < len(t_old):
                            x = x - t_old[k]
                        new_t.append(x)
                fields.append(new_h)
                h_now, h_old, t_now, t_old = new_h, h_now, new_t, t_now
            return corrections, fields

        more_laps, _ = march(0, False)
        _, more_adjoints = march(steps, True)
        for k, z in enumerate(at):
            total = None
            for n in range(steps):
                a = laps[n][z]
                if k < len(more_laps[n]):
                    a = a + more_laps[n][k]
                b = adjoints[steps - 1 - n][z]
                if k < len(more_adjoints[steps - 1 - n]):
                    b = b + more_adjoints[steps - 1 - n][k]
                total = a * b if total is None else total + a * b
            store(z, total)

    start, live = offset[0], count[0]
    odd = lax.rem(start + lax.axis_index("shot"), 2)
    zero = jnp.zeros((depth * span, size), jnp.float32)
    half = blocks // 2

    @pl.loop(0, half)
    def _(i):
        for ref, j in ((own, 2 * i + odd), (other, 2 * i + 1 - odd)):
            k = lax.div(start + j, 2)
            ref[k] = jnp.where(j < live, blocked[j], 0.0)
            ref[lax.rem(k + half, blocks)] = zero


def shards(vel, wave, wave_old, adj, adj_old, residuals, offset, count):
    _, depth, width, size = vel.shape
    steps = residuals.shape[1]
    shots, doms = lax.axis_size("shot"), lax.axis_size("dom")
    blocks = shots // 2
    span = width // blocks
    f32 = jnp.float32
    hbm = pl.BlockSpec(memory_space=pltpu.HBM)
    smem = pl.BlockSpec(memory_space=pltpu.SMEM)
    vmem = pl.BlockSpec(memory_space=pltpu.VMEM)
    room = pltpu.CompilerParams(vmem_limit_bytes=24 * 2**20)
    message = jax.ShapeDtypeStruct((2 * steps + 2, width, size), f32)
    field = jax.ShapeDtypeStruct((depth, width, size), f32)
    block = jax.ShapeDtypeStruct((blocks, depth * span, size), f32)

    up, down = pl.pallas_call(
        functools.partial(edges, steps, depth),
        out_shape=(message, message),
        in_specs=[hbm] * 5,
        out_specs=(vmem, vmem),
        scratch_shapes=[pltpu.VMEM((2, steps, width, size), f32)] * 5 + [pltpu.SemaphoreType.DMA((5, 2))],
        compiler_params=pltpu.CompilerParams(vmem_limit_bytes=53 * 2**20),
    )(vel, wave, wave_old, adj, adj_old)

    low = lax.ppermute(up, "dom", [(i, i + 1) for i in range(doms - 1)])
    high = lax.ppermute(down, "dom", [(i + 1, i) for i in range(doms - 1)])

    inner = pl.pallas_call(
        functools.partial(slab, steps, depth),
        out_shape=(field,) * (2 * steps + 1),
        in_specs=[vmem] * 6,
        out_specs=(vmem,) * (2 * steps + 1),
        scratch_shapes=[pltpu.VMEM((depth + 2, width, size), f32)] * 4,
        cost_estimate=pl.CostEstimate(flops=40_000_000, bytes_accessed=16_000_000, transcendentals=0),
        compiler_params=room,
    )(vel, wave, wave_old, adj, adj_old, residuals)

    own, other = pl.pallas_call(
        functools.partial(finish, steps, depth, blocks),
        out_shape=(block, block),
        in_specs=[smem, smem] + [vmem] * (6 + 2 * steps),
        out_specs=(vmem, vmem),
        scratch_shapes=[pltpu.VMEM((blocks, depth * span, size), f32)],
        compiler_params=room,
    )(offset, count, vel, up, down, low, high, *inner)

    pair = [(s, s + 1 - 2 * (s % 2)) for s in range(shots)]
    both = own + lax.ppermute(other, "shot", pair)
    groups = [[2 * k + c for k in range(blocks)] for c in range(2)]
    parts = lax.all_to_all(both, "shot", 0, 0, tiled=True, axis_index_groups=groups)
    return jnp.sum(parts, axis=0).reshape(1, depth, span, size)


def solution(mesh):
    field = P("shot", "dom", None, None)
    placed = (field,) * 5 + (P("shot", None, None, None), P("shot"), P("shot"))
    return jax.shard_map(shards, mesh=mesh, in_specs=placed, out_specs=field, check_vma=False)
```

```python
import functools

import jax
import jax.numpy as jnp
from jax import lax
from jax.experimental import pallas as pl
from jax.experimental.pallas import tpu as pltpu
from jax.sharding import PartitionSpec as P


class Lateral:
    def __init__(self, width, size):
        row = lax.broadcasted_iota(jnp.int32, (width, size), 0)
        column = lax.broadcasted_iota(jnp.int32, (width, size), 1)
        self.width, self.size = width, size
        self.top, self.bottom = row == 0, row == width - 1
        self.first, self.last = column == 0, column == size - 1

    def __call__(self, middle):
        above = jnp.where(self.top, 0.0, pltpu.roll(middle, 1, 0))
        below = jnp.where(self.bottom, 0.0, pltpu.roll(middle, self.width - 1, 0))
        left = jnp.where(self.first, 0.0, pltpu.roll(middle, 1, 1))
        right = jnp.where(self.last, 0.0, pltpu.roll(middle, self.size - 1, 1))
        return (above + below) + (left + right) - 6.0 * middle


def edges(steps, depth, vel, wave, wave_old, adj, adj_old, up, down, *scratch):
    _, _, width, size = vel.shape
    lateral = Lateral(width, size)
    fetched, sems = scratch[:5], scratch[5]
    copies = []
    for i, (ref, held) in enumerate(zip((vel, wave, wave_old, adj, adj_old), fetched)):
        for side, begin in enumerate((0, depth - steps)):
            copies.append(pltpu.make_async_copy(ref.at[0, pl.ds(begin, steps)], held.at[side], sems.at[i, side]))
    for copy in copies:
        copy.start()
    for copy in copies:
        copy.wait()
    vel, wave, wave_old, adj, adj_old = fetched
    for out, top in ((down, False), (up, True)):
        side = int(top)
        at = [steps - 1 - k if top else k for k in range(steps)]
        v = [vel[side, z] for z in at]
        out[2 * steps] = v[0]
        out[2 * steps + 1] = v[1]
        now, old = [wave[side, z] for z in at], [wave_old[side, z] for z in at[:-1]]
        out[0] = now[0]
        for step in range(1, steps):
            new = []
            for k in range(steps - step):
                lap = lateral(now[k]) + now[k + 1]
                if k > 0:
                    lap = lap + now[k - 1]
                new.append(2.0 * now[k] - old[k] + v[k] * lap)
            now, old = new, now
            out[step] = now[0]
        now, old = [adj[side, z] for z in at], [adj_old[side, z] for z in at[:-1]]
        scaled = [c * q for c, q in zip(v, now)]
        out[steps] = scaled[0]
        for step in range(1, steps):
            new = []
            for k in range(steps - step):
                lap = lateral(scaled[k]) + scaled[k + 1]
                if k > 0:
                    lap = lap + scaled[k - 1]
                new.append(2.0 * now[k] - old[k] + lap)
            now, old = new, now
            scaled = [c * q for c, q in zip(v, now)]
            out[steps + step] = scaled[0]


def slab(steps, depth, *refs):
    vel, wave, wave_old, adj, adj_old, residuals = [ref.at[0] for ref in refs[:6]]
    refs = refs[6:]
    laps, adjoints, img = refs[:steps], refs[steps : 2 * steps], refs[2 * steps]
    refs = refs[2 * steps + 1 :]
    ps, ws = refs[:2], refs[2:]
    _, width, size = vel.shape
    lateral = Lateral(width, size)
    blank = jnp.zeros((width, size), jnp.float32)
    for ref in (*ps, *ws):
        ref[0] = blank
        ref[depth + 1] = blank

    for z in range(depth):
        ps[0][z + 1] = wave[z]
        ws[0][z + 1] = vel[z] * adj[z]

    surface = jnp.where(lax.axis_index("dom") == 0, 1.0, 0.0)
    fields = (adj_old, adj, *adjoints)
    for step in range(steps):
        source, target = ws[step % 2], ws[(step + 1) % 2]
        old, now, new = fields[step : step + 3]
        for z in range(depth):
            lap = lateral(source[z + 1]) + (source[z] + source[z + 2])
            q = 2.0 * now[z] - old[z] + lap
            if z == 0:
                q = q + surface * residuals[step]
            new[z] = q
            if step < steps - 1:
                target[z + 1] = vel[z] * q

    for step in range(steps):
        source, target = ps[step % 2], ps[(step + 1) % 2]
        for z in range(depth):
            middle = source[z + 1]
            lap = lateral(middle) + (source[z] + source[z + 2])
            term = lap * adjoints[steps - 1 - step][z]
            if step > 0:
                term = term + img[z]
            laps[step][z] = lap
            img[z] = term
            if step < steps - 1:
                old = wave_old[z] if step == 0 else target[z + 1]
                target[z + 1] = 2.0 * middle - old + vel[z] * lap


def finish(steps, depth, blocks, *refs):
    offset, count, vel, up, down, low, high = refs[:7]
    vel = vel.at[0]
    laps, adjoints, img = refs[7 : 7 + steps], refs[7 + steps : 7 + 2 * steps], refs[7 + 2 * steps]
    own, other, blocked = refs[8 + 2 * steps :]
    _, width, size = vel.shape
    lateral = Lateral(width, size)
    span = width // blocks

    def store(z, plane):
        for j in range(blocks):
            blocked[j, z * span : (z + 1) * span, :] = plane[j * span : (j + 1) * span, :]

    for z in range(steps, depth - steps):
        store(z, img[z])

    for sent, got, top in ((down, low, False), (up, high, True)):
        at = [depth - 1 - k if top else k for k in range(steps)]
        here = [vel[z] for z in at]
        there = [got[2 * steps], got[2 * steps + 1]]

        def march(first, scale_field):
            f = [sent[first + n] for n in range(steps)]
            g = [got[first + n] for n in range(steps)]
            corrections, fields = [], []
            h_now, h_old, t_now, t_old = [], [], [], []
            for step in range(steps):
                if scale_field:
                    hs = [c * x for c, x in zip(here, h_now)]
                    ts = [c * x for c, x in zip(there, t_now)]
                else:
                    hs, ts = h_now, t_now
                laps_here = []
                for k in range(step + 1):
                    lap = g[step] if k == 0 else hs[k - 1]
                    if k == 0 and step > 0:
                        lap = lap + ts[0]
                    if k < len(hs):
                        lap = lap + lateral(hs[k])
                    if k + 1 < len(hs):
                        lap = lap + hs[k + 1]
                    laps_here.append(lap)
                corrections.append(laps_here)
                last = step == steps - 1
                new_h, new_t = [], []
                if scale_field or not last:
                    for k, lap in enumerate(laps_here):
                        x = lap if scale_field else here[k] * lap
                        if k < len(h_now):
                            x = x + 2.0 * h_now[k]
                        if k < len(h_old):
                            x = x - h_old[k]
                        new_h.append(x)
                if not last:
                    for k in range(min(step + 1, steps - 1 - step)):
                        lap = f[step] if k == 0 else ts[k - 1]
                        if k == 0 and step > 0:
                            lap = lap + hs[0]
                        if k < len(ts):
                            lap = lap + lateral(ts[k])
                        if k + 1 < len(ts):
                            lap = lap + ts[k + 1]
                        x = lap if scale_field else there[k] * lap
                        if k < len(t_now):
                            x = x + 2.0 * t_now[k]
                        if k < len(t_old):
                            x = x - t_old[k]
                        new_t.append(x)
                fields.append(new_h)
                h_now, h_old, t_now, t_old = new_h, h_now, new_t, t_now
            return corrections, fields

        more_laps, _ = march(0, False)
        _, more_adjoints = march(steps, True)
        for k, z in enumerate(at):
            total = None
            for n in range(steps):
                a = laps[n][z]
                if k < len(more_laps[n]):
                    a = a + more_laps[n][k]
                b = adjoints[steps - 1 - n][z]
                if k < len(more_adjoints[steps - 1 - n]):
                    b = b + more_adjoints[steps - 1 - n][k]
                total = a * b if total is None else total + a * b
            store(z, total)

    start, live = offset[0], count[0]
    odd = lax.rem(start + lax.axis_index("shot"), 2)
    zero = jnp.zeros((depth * span, size), jnp.float32)
    half = blocks // 2

    @pl.loop(0, half)
    def _(i):
        for ref, j in ((own, 2 * i + odd), (other, 2 * i + 1 - odd)):
            k = lax.div(start + j, 2)
            ref[k] = jnp.where(j < live, blocked[j], 0.0)
            ref[lax.rem(k + half, blocks)] = zero


def totals(parts, kept, sent):
    side = lax.rem(lax.div(lax.axis_index("shot"), 2), 2)
    for out, at in ((sent, 1 - side), (kept, side)):
        total = parts[0, at]
        for source in range(1, parts.shape[0]):
            total = total + parts[source, at]
        out[...] = total


def shards(vel, wave, wave_old, adj, adj_old, residuals, offset, count):
    _, depth, width, size = vel.shape
    steps = residuals.shape[1]
    shots, doms = lax.axis_size("shot"), lax.axis_size("dom")
    blocks = shots // 2
    span = width // blocks
    f32 = jnp.float32
    hbm = pl.BlockSpec(memory_space=pltpu.HBM)
    smem = pl.BlockSpec(memory_space=pltpu.SMEM)
    vmem = pl.BlockSpec(memory_space=pltpu.VMEM)
    room = pltpu.CompilerParams(vmem_limit_bytes=24 * 2**20)
    message = jax.ShapeDtypeStruct((2 * steps + 2, width, size), f32)
    field = jax.ShapeDtypeStruct((depth, width, size), f32)
    block = jax.ShapeDtypeStruct((blocks, depth * span, size), f32)

    up, down = pl.pallas_call(
        functools.partial(edges, steps, depth),
        out_shape=(message, message),
        in_specs=[hbm] * 5,
        out_specs=(vmem, vmem),
        scratch_shapes=[pltpu.VMEM((2, steps, width, size), f32)] * 5 + [pltpu.SemaphoreType.DMA((5, 2))],
        compiler_params=pltpu.CompilerParams(vmem_limit_bytes=53 * 2**20),
    )(vel, wave, wave_old, adj, adj_old)

    low = lax.ppermute(up, "dom", [(i, i + 1) for i in range(doms - 1)])
    high = lax.ppermute(down, "dom", [(i + 1, i) for i in range(doms - 1)])

    inner = pl.pallas_call(
        functools.partial(slab, steps, depth),
        out_shape=(field,) * (2 * steps + 1),
        in_specs=[vmem] * 6,
        out_specs=(vmem,) * (2 * steps + 1),
        scratch_shapes=[pltpu.VMEM((depth + 2, width, size), f32)] * 4,
        cost_estimate=pl.CostEstimate(flops=40_000_000, bytes_accessed=16_000_000, transcendentals=0),
        compiler_params=room,
    )(vel, wave, wave_old, adj, adj_old, residuals)

    own, other = pl.pallas_call(
        functools.partial(finish, steps, depth, blocks),
        out_shape=(block, block),
        in_specs=[smem, smem] + [vmem] * (6 + 2 * steps),
        out_specs=(vmem, vmem),
        scratch_shapes=[pltpu.VMEM((blocks, depth * span, size), f32)],
        compiler_params=room,
    )(offset, count, vel, up, down, low, high, *inner)

    pair = [(s, s + 1 - 2 * (s % 2)) for s in range(shots)]
    both = own + lax.ppermute(other, "shot", pair)
    rows = depth * span
    layers = shots // 4
    groups = [[4 * z + r for z in range(layers)] for r in range(4)]
    parts = lax.all_to_all(
        both.reshape(layers, 2, rows, size), "shot", 0, 0, tiled=True, axis_index_groups=groups
    )
    part = jax.ShapeDtypeStruct((rows, size), f32)
    kept, sent = pl.pallas_call(
        totals, out_shape=(part, part), in_specs=[vmem], out_specs=(vmem, vmem), compiler_params=room
    )(parts)
    across = [(s, s + 2 - 4 * (s // 2 % 2)) for s in range(shots)]
    return (kept + lax.ppermute(sent, "shot", across)).reshape(1, depth, span, size)


def solution(mesh):
    field = P("shot", "dom", None, None)
    placed = (field,) * 5 + (P("shot", None, None, None), P("shot"), P("shot"))
    return jax.shard_map(shards, mesh=mesh, in_specs=placed, out_specs=field, check_vma=False)
```

```python
import functools

import jax
import jax.numpy as jnp
from jax import lax
from jax.experimental import pallas as pl
from jax.experimental.pallas import tpu as pltpu
from jax.sharding import PartitionSpec as P


class Lateral:
    def __init__(self, width, size):
        row = lax.broadcasted_iota(jnp.int32, (width, size), 0)
        column = lax.broadcasted_iota(jnp.int32, (width, size), 1)
        self.width, self.size = width, size
        self.top, self.bottom = row == 0, row == width - 1
        self.first, self.last = column == 0, column == size - 1

    def __call__(self, middle):
        above = jnp.where(self.top, 0.0, pltpu.roll(middle, 1, 0))
        below = jnp.where(self.bottom, 0.0, pltpu.roll(middle, self.width - 1, 0))
        left = jnp.where(self.first, 0.0, pltpu.roll(middle, 1, 1))
        right = jnp.where(self.last, 0.0, pltpu.roll(middle, self.size - 1, 1))
        return (above + below) + (left + right) - 6.0 * middle


def sides():
    odd = lax.rem(lax.axis_index("dom"), 2)
    return odd, 1 - odd


def edges(steps, depth, vel, wave, wave_old, adj, adj_old, first, second, *scratch):
    _, _, width, size = vel.shape
    lateral = Lateral(width, size)
    fetched, sems = scratch[:5], scratch[5]
    copies = [
        [
            pltpu.make_async_copy(ref.at[0, pl.ds(side * (depth - steps), steps)], held.at[at], sems.at[at, i])
            for i, (ref, held) in enumerate(zip((vel, wave, wave_old, adj, adj_old), fetched))
        ]
        for at, side in enumerate(sides())
    ]
    for copy in copies[0] + copies[1]:
        copy.start()
    vel, wave, wave_old, adj, adj_old = fetched
    for side, (out, top) in enumerate(zip((first, second), sides())):
        for copy in copies[side]:
            copy.wait()
        at = [k + top * (steps - 1 - 2 * k) for k in range(steps)]
        v = [vel[side, z] for z in at]
        out[2 * steps] = v[0]
        out[2 * steps + 1] = v[1]
        now, old = [wave[side, z] for z in at], [wave_old[side, z] for z in at[:-1]]
        out[0] = now[0]
        for step in range(1, steps):
            new = []
            for k in range(steps - step):
                lap = lateral(now[k]) + now[k + 1]
                if k > 0:
                    lap = lap + now[k - 1]
                new.append(2.0 * now[k] - old[k] + v[k] * lap)
            now, old = new, now
            out[step] = now[0]
        now, old = [adj[side, z] for z in at], [adj_old[side, z] for z in at[:-1]]
        scaled = [c * q for c, q in zip(v, now)]
        out[steps] = scaled[0]
        for step in range(1, steps):
            new = []
            for k in range(steps - step):
                lap = lateral(scaled[k]) + scaled[k + 1]
                if k > 0:
                    lap = lap + scaled[k - 1]
                new.append(2.0 * now[k] - old[k] + lap)
            now, old = new, now
            scaled = [c * q for c, q in zip(v, now)]
            out[steps + step] = scaled[0]


def slab(steps, depth, *refs):
    vel, wave, wave_old, adj, adj_old, residuals = [ref.at[0] for ref in refs[:6]]
    refs = refs[6:]
    laps, adjoints, img = refs[:steps], refs[steps : 2 * steps], refs[2 * steps]
    refs = refs[2 * steps + 1 :]
    ps, ws = refs[:2], refs[2:]
    _, width, size = vel.shape
    lateral = Lateral(width, size)
    blank = jnp.zeros((width, size), jnp.float32)
    for ref in (*ps, *ws):
        ref[0] = blank
        ref[depth + 1] = blank

    for z in range(depth):
        ps[0][z + 1] = wave[z]
        ws[0][z + 1] = vel[z] * adj[z]

    surface = jnp.where(lax.axis_index("dom") == 0, 1.0, 0.0)
    fields = (adj_old, adj, *adjoints)
    for step in range(steps):
        source, target = ws[step % 2], ws[(step + 1) % 2]
        old, now, new = fields[step : step + 3]
        for z in range(depth):
            lap = lateral(source[z + 1]) + (source[z] + source[z + 2])
            q = 2.0 * now[z] - old[z] + lap
            if z == 0:
                q = q + surface * residuals[step]
            new[z] = q
            if step < steps - 1:
                target[z + 1] = vel[z] * q

    for step in range(steps):
        source, target = ps[step % 2], ps[(step + 1) % 2]
        for z in range(depth):
            middle = source[z + 1]
            lap = lateral(middle) + (source[z] + source[z + 2])
            term = lap * adjoints[steps - 1 - step][z]
            if step > 0:
                term = term + img[z]
            laps[step][z] = lap
            img[z] = term
            if step < steps - 1:
                old = wave_old[z] if step == 0 else target[z + 1]
                target[z + 1] = 2.0 * middle - old + vel[z] * lap


def finish(steps, depth, blocks, *refs):
    offset, count, vel, first, second, from_first, from_second = refs[:7]
    vel = vel.at[0]
    laps, adjoints, img = refs[7 : 7 + steps], refs[7 + steps : 7 + 2 * steps], refs[7 + 2 * steps]
    own, other, blocked, outer = refs[8 + 2 * steps :]
    _, width, size = vel.shape
    lateral = Lateral(width, size)
    span = width // blocks

    def store(z, plane):
        for j in range(blocks):
            blocked[j, z * span : (z + 1) * span, :] = plane[j * span : (j + 1) * span, :]

    for z in range(steps, depth - steps):
        store(z, img[z])

    for sent, got, top in zip((first, second), (from_first, from_second), sides()):
        at = [k + top * (depth - 1 - 2 * k) for k in range(steps)]
        here = [vel[z] for z in at]
        there = [got[2 * steps], got[2 * steps + 1]]

        def march(first, scale_field):
            f = [sent[first + n] for n in range(steps)]
            g = [got[first + n] for n in range(steps)]
            corrections, fields = [], []
            h_now, h_old, t_now, t_old = [], [], [], []
            for step in range(steps):
                if scale_field:
                    hs = [c * x for c, x in zip(here, h_now)]
                    ts = [c * x for c, x in zip(there, t_now)]
                else:
                    hs, ts = h_now, t_now
                laps_here = []
                for k in range(step + 1):
                    lap = g[step] if k == 0 else hs[k - 1]
                    if k == 0 and step > 0:
                        lap = lap + ts[0]
                    if k < len(hs):
                        lap = lap + lateral(hs[k])
                    if k + 1 < len(hs):
                        lap = lap + hs[k + 1]
                    laps_here.append(lap)
                corrections.append(laps_here)
                last = step == steps - 1
                new_h, new_t = [], []
                if scale_field or not last:
                    for k, lap in enumerate(laps_here):
                        x = lap if scale_field else here[k] * lap
                        if k < len(h_now):
                            x = x + 2.0 * h_now[k]
                        if k < len(h_old):
                            x = x - h_old[k]
                        new_h.append(x)
                if not last:
                    for k in range(min(step + 1, steps - 1 - step)):
                        lap = f[step] if k == 0 else ts[k - 1]
                        if k == 0 and step > 0:
                            lap = lap + hs[0]
                        if k < len(ts):
                            lap = lap + lateral(ts[k])
                        if k + 1 < len(ts):
                            lap = lap + ts[k + 1]
                        x = lap if scale_field else there[k] * lap
                        if k < len(t_now):
                            x = x + 2.0 * t_now[k]
                        if k < len(t_old):
                            x = x - t_old[k]
                        new_t.append(x)
                fields.append(new_h)
                h_now, h_old, t_now, t_old = new_h, h_now, new_t, t_now
            return corrections, fields

        more_laps, _ = march(0, False)
        _, more_adjoints = march(steps, True)
        for k, z in enumerate(at):
            total = None
            for n in range(steps):
                a = laps[n][z]
                if k < len(more_laps[n]):
                    a = a + more_laps[n][k]
                b = adjoints[steps - 1 - n][z]
                if k < len(more_adjoints[steps - 1 - n]):
                    b = b + more_adjoints[steps - 1 - n][k]
                total = a * b if total is None else total + a * b
            outer[z] = total

    for z in (*range(steps), *range(depth - steps, depth)):
        store(z, outer[z])

    start, live = offset[0], count[0]
    odd = lax.rem(start + lax.axis_index("shot"), 2)
    zero = jnp.zeros((depth * span, size), jnp.float32)
    half = blocks // 2

    @pl.loop(0, half)
    def _(i):
        for ref, j in ((own, 2 * i + odd), (other, 2 * i + 1 - odd)):
            k = lax.div(start + j, 2)
            ref[k] = jnp.where(j < live, blocked[j], 0.0)
            ref[lax.rem(k + half, blocks)] = zero


def shards(vel, wave, wave_old, adj, adj_old, residuals, offset, count):
    _, depth, width, size = vel.shape
    steps = residuals.shape[1]
    shots, doms = lax.axis_size("shot"), lax.axis_size("dom")
    blocks = shots // 2
    span = width // blocks
    f32 = jnp.float32
    hbm = pl.BlockSpec(memory_space=pltpu.HBM)
    smem = pl.BlockSpec(memory_space=pltpu.SMEM)
    vmem = pl.BlockSpec(memory_space=pltpu.VMEM)
    room = pltpu.CompilerParams(vmem_limit_bytes=24 * 2**20)
    message = jax.ShapeDtypeStruct((2 * steps + 2, width, size), f32)
    field = jax.ShapeDtypeStruct((depth, width, size), f32)
    block = jax.ShapeDtypeStruct((blocks, depth * span, size), f32)

    first, second = pl.pallas_call(
        functools.partial(edges, steps, depth),
        out_shape=(message, message),
        in_specs=[hbm] * 5,
        out_specs=(vmem, vmem),
        scratch_shapes=[pltpu.VMEM((2, steps, width, size), f32)] * 5 + [pltpu.SemaphoreType.DMA((2, 5))],
        compiler_params=pltpu.CompilerParams(vmem_limit_bytes=53 * 2**20),
    )(vel, wave, wave_old, adj, adj_old)

    def exchange(message, begin):
        lower = range(begin, doms - 1, 2)
        return lax.ppermute(message, "dom", [(i, i + 1) for i in lower] + [(i + 1, i) for i in lower])

    from_first, from_second = exchange(first, 1), exchange(second, 0)

    inner = pl.pallas_call(
        functools.partial(slab, steps, depth),
        out_shape=(field,) * (2 * steps + 1),
        in_specs=[vmem] * 6,
        out_specs=(vmem,) * (2 * steps + 1),
        scratch_shapes=[pltpu.VMEM((depth + 2, width, size), f32)] * 4,
        cost_estimate=pl.CostEstimate(flops=40_000_000, bytes_accessed=16_000_000, transcendentals=0),
        compiler_params=room,
    )(vel, wave, wave_old, adj, adj_old, residuals)

    own, other = pl.pallas_call(
        functools.partial(finish, steps, depth, blocks),
        out_shape=(block, block),
        in_specs=[smem, smem] + [vmem] * (6 + 2 * steps),
        out_specs=(vmem, vmem),
        scratch_shapes=[pltpu.VMEM((blocks, depth * span, size), f32), pltpu.VMEM((depth, width, size), f32)],
        compiler_params=room,
    )(offset, count, vel, first, second, from_first, from_second, *inner)

    pair = [(s, s + 1 - 2 * (s % 2)) for s in range(shots)]
    both = own + lax.ppermute(other, "shot", pair)
    groups = [[2 * k + c for k in range(blocks)] for c in range(2)]
    parts = lax.all_to_all(both, "shot", 0, 0, tiled=True, axis_index_groups=groups)
    return jnp.sum(parts, axis=0).reshape(1, depth, span, size)


def solution(mesh):
    field = P("shot", "dom", None, None)
    placed = (field,) * 5 + (P("shot", None, None, None), P("shot"), P("shot"))
    return jax.shard_map(shards, mesh=mesh, in_specs=placed, out_specs=field, check_vma=False)
```

```python
import functools

import jax
import jax.numpy as jnp
from jax import lax
from jax.experimental import pallas as pl
from jax.experimental.pallas import tpu as pltpu
from jax.sharding import PartitionSpec as P


class Lateral:
    def __init__(self, width, size):
        row = lax.broadcasted_iota(jnp.int32, (width, size), 0)
        column = lax.broadcasted_iota(jnp.int32, (width, size), 1)
        self.width, self.size = width, size
        self.top, self.bottom = row == 0, row == width - 1
        self.first, self.last = column == 0, column == size - 1

    def __call__(self, middle):
        above = jnp.where(self.top, 0.0, pltpu.roll(middle, 1, 0))
        below = jnp.where(self.bottom, 0.0, pltpu.roll(middle, self.width - 1, 0))
        left = jnp.where(self.first, 0.0, pltpu.roll(middle, 1, 1))
        right = jnp.where(self.last, 0.0, pltpu.roll(middle, self.size - 1, 1))
        return (above + below) + (left + right) - 6.0 * middle


def sides():
    odd = lax.rem(lax.axis_index("dom"), 2)
    return 1 - odd, odd


def edges(steps, depth, vel, wave, wave_old, adj, adj_old, first, second, *scratch):
    _, _, width, size = vel.shape
    lateral = Lateral(width, size)
    fetched, sems = scratch[:5], scratch[5]
    copies = [
        [
            pltpu.make_async_copy(ref.at[0, pl.ds(side * (depth - steps), steps)], held.at[at], sems.at[at, i])
            for i, (ref, held) in enumerate(zip((vel, wave, wave_old, adj, adj_old), fetched))
        ]
        for at, side in enumerate(sides())
    ]
    for copy in copies[0] + copies[1]:
        copy.start()
    vel, wave, wave_old, adj, adj_old = fetched
    for side, (out, top) in enumerate(zip((first, second), sides())):
        for copy in copies[side]:
            copy.wait()
        at = [k + top * (steps - 1 - 2 * k) for k in range(steps)]
        v = [vel[side, z] for z in at]
        out[2 * steps] = v[0]
        out[2 * steps + 1] = v[1]
        now, old = [wave[side, z] for z in at], [wave_old[side, z] for z in at[:-1]]
        out[0] = now[0]
        for step in range(1, steps):
            new = []
            for k in range(steps - step):
                lap = lateral(now[k]) + now[k + 1]
                if k > 0:
                    lap = lap + now[k - 1]
                new.append(2.0 * now[k] - old[k] + v[k] * lap)
            now, old = new, now
            out[step] = now[0]
        now, old = [adj[side, z] for z in at], [adj_old[side, z] for z in at[:-1]]
        scaled = [c * q for c, q in zip(v, now)]
        out[steps] = scaled[0]
        for step in range(1, steps):
            new = []
            for k in range(steps - step):
                lap = lateral(scaled[k]) + scaled[k + 1]
                if k > 0:
                    lap = lap + scaled[k - 1]
                new.append(2.0 * now[k] - old[k] + lap)
            now, old = new, now
            scaled = [c * q for c, q in zip(v, now)]
            out[steps + step] = scaled[0]


def slab(steps, depth, *refs):
    vel, wave, wave_old, adj, adj_old, residuals = [ref.at[0] for ref in refs[:6]]
    refs = refs[6:]
    laps, adjoints, img = refs[:steps], refs[steps : 2 * steps], refs[2 * steps]
    refs = refs[2 * steps + 1 :]
    ps, ws = refs[:2], refs[2:]
    _, width, size = vel.shape
    lateral = Lateral(width, size)
    blank = jnp.zeros((width, size), jnp.float32)
    for ref in (*ps, *ws):
        ref[0] = blank
        ref[depth + 1] = blank

    for z in range(depth):
        ps[0][z + 1] = wave[z]
        ws[0][z + 1] = vel[z] * adj[z]

    surface = jnp.where(lax.axis_index("dom") == 0, 1.0, 0.0)
    fields = (adj_old, adj, *adjoints)
    for step in range(steps):
        source, target = ws[step % 2], ws[(step + 1) % 2]
        old, now, new = fields[step : step + 3]
        for z in range(depth):
            lap = lateral(source[z + 1]) + (source[z] + source[z + 2])
            q = 2.0 * now[z] - old[z] + lap
            if z == 0:
                q = q + surface * residuals[step]
            new[z] = q
            if step < steps - 1:
                target[z + 1] = vel[z] * q

    for step in range(steps):
        source, target = ps[step % 2], ps[(step + 1) % 2]
        for z in range(depth):
            middle = source[z + 1]
            lap = lateral(middle) + (source[z] + source[z + 2])
            term = lap * adjoints[steps - 1 - step][z]
            if step > 0:
                term = term + img[z]
            laps[step][z] = lap
            img[z] = term
            if step < steps - 1:
                old = wave_old[z] if step == 0 else target[z + 1]
                target[z + 1] = 2.0 * middle - old + vel[z] * lap


def finish(steps, depth, blocks, *refs):
    offset, count, vel, first, second, from_first, from_second = refs[:7]
    vel = vel.at[0]
    laps, adjoints, img = refs[7 : 7 + steps], refs[7 + steps : 7 + 2 * steps], refs[7 + 2 * steps]
    own, other, blocked, outer = refs[8 + 2 * steps :]
    _, width, size = vel.shape
    lateral = Lateral(width, size)
    span = width // blocks

    def store(z, plane):
        for j in range(blocks):
            blocked[j, z * span : (z + 1) * span, :] = plane[j * span : (j + 1) * span, :]

    for z in range(steps, depth - steps):
        store(z, img[z])

    for sent, got, top in zip((first, second), (from_first, from_second), sides()):
        at = [k + top * (depth - 1 - 2 * k) for k in range(steps)]
        here = [vel[z] for z in at]
        there = [got[2 * steps], got[2 * steps + 1]]

        def march(first, scale_field):
            f = [sent[first + n] for n in range(steps)]
            g = [got[first + n] for n in range(steps)]
            corrections, fields = [], []
            h_now, h_old, t_now, t_old = [], [], [], []
            for step in range(steps):
                if scale_field:
                    hs = [c * x for c, x in zip(here, h_now)]
                    ts = [c * x for c, x in zip(there, t_now)]
                else:
                    hs, ts = h_now, t_now
                laps_here = []
                for k in range(step + 1):
                    lap = g[step] if k == 0 else hs[k - 1]
                    if k == 0 and step > 0:
                        lap = lap + ts[0]
                    if k < len(hs):
                        lap = lap + lateral(hs[k])
                    if k + 1 < len(hs):
                        lap = lap + hs[k + 1]
                    laps_here.append(lap)
                corrections.append(laps_here)
                last = step == steps - 1
                new_h, new_t = [], []
                if scale_field or not last:
                    for k, lap in enumerate(laps_here):
                        x = lap if scale_field else here[k] * lap
                        if k < len(h_now):
                            x = x + 2.0 * h_now[k]
                        if k < len(h_old):
                            x = x - h_old[k]
                        new_h.append(x)
                if not last:
                    for k in range(min(step + 1, steps - 1 - step)):
                        lap = f[step] if k == 0 else ts[k - 1]
                        if k == 0 and step > 0:
                            lap = lap + hs[0]
                        if k < len(ts):
                            lap = lap + lateral(ts[k])
                        if k + 1 < len(ts):
                            lap = lap + ts[k + 1]
                        x = lap if scale_field else there[k] * lap
                        if k < len(t_now):
                            x = x + 2.0 * t_now[k]
                        if k < len(t_old):
                            x = x - t_old[k]
                        new_t.append(x)
                fields.append(new_h)
                h_now, h_old, t_now, t_old = new_h, h_now, new_t, t_now
            return corrections, fields

        more_laps, _ = march(0, False)
        _, more_adjoints = march(steps, True)
        for k, z in enumerate(at):
            total = None
            for n in range(steps):
                a = laps[n][z]
                if k < len(more_laps[n]):
                    a = a + more_laps[n][k]
                b = adjoints[steps - 1 - n][z]
                if k < len(more_adjoints[steps - 1 - n]):
                    b = b + more_adjoints[steps - 1 - n][k]
                total = a * b if total is None else total + a * b
            outer[z] = total

    for z in (*range(steps), *range(depth - steps, depth)):
        store(z, outer[z])

    start, live = offset[0], count[0]
    odd = lax.rem(start + lax.axis_index("shot"), 2)
    zero = jnp.zeros((depth * span, size), jnp.float32)
    half = blocks // 2

    @pl.loop(0, half)
    def _(i):
        for ref, j in ((own, 2 * i + odd), (other, 2 * i + 1 - odd)):
            k = lax.div(start + j, 2)
            ref[k] = jnp.where(j < live, blocked[j], 0.0)
            ref[lax.rem(k + half, blocks)] = zero


def shards(vel, wave, wave_old, adj, adj_old, residuals, offset, count):
    _, depth, width, size = vel.shape
    steps = residuals.shape[1]
    shots, doms = lax.axis_size("shot"), lax.axis_size("dom")
    blocks = shots // 2
    span = width // blocks
    f32 = jnp.float32
    hbm = pl.BlockSpec(memory_space=pltpu.HBM)
    smem = pl.BlockSpec(memory_space=pltpu.SMEM)
    vmem = pl.BlockSpec(memory_space=pltpu.VMEM)
    room = pltpu.CompilerParams(vmem_limit_bytes=24 * 2**20)
    message = jax.ShapeDtypeStruct((2 * steps + 2, width, size), f32)
    field = jax.ShapeDtypeStruct((depth, width, size), f32)
    block = jax.ShapeDtypeStruct((blocks, depth * span, size), f32)

    first, second = pl.pallas_call(
        functools.partial(edges, steps, depth),
        out_shape=(message, message),
        in_specs=[hbm] * 5,
        out_specs=(vmem, vmem),
        scratch_shapes=[pltpu.VMEM((2, steps, width, size), f32)] * 5 + [pltpu.SemaphoreType.DMA((2, 5))],
        compiler_params=pltpu.CompilerParams(vmem_limit_bytes=53 * 2**20),
    )(vel, wave, wave_old, adj, adj_old)

    def exchange(message, begin):
        lower = range(begin, doms - 1, 2)
        return lax.ppermute(message, "dom", [(i, i + 1) for i in lower] + [(i + 1, i) for i in lower])

    from_first, from_second = exchange(first, 0), exchange(second, 1)

    inner = pl.pallas_call(
        functools.partial(slab, steps, depth),
        out_shape=(field,) * (2 * steps + 1),
        in_specs=[vmem] * 6,
        out_specs=(vmem,) * (2 * steps + 1),
        scratch_shapes=[pltpu.VMEM((depth + 2, width, size), f32)] * 4,
        cost_estimate=pl.CostEstimate(flops=40_000_000, bytes_accessed=16_000_000, transcendentals=0),
        compiler_params=room,
    )(vel, wave, wave_old, adj, adj_old, residuals)

    own, other = pl.pallas_call(
        functools.partial(finish, steps, depth, blocks),
        out_shape=(block, block),
        in_specs=[smem, smem] + [vmem] * (6 + 2 * steps),
        out_specs=(vmem, vmem),
        scratch_shapes=[pltpu.VMEM((blocks, depth * span, size), f32), pltpu.VMEM((depth, width, size), f32)],
        compiler_params=room,
    )(offset, count, vel, first, second, from_first, from_second, *inner)

    pair = [(s, s + 1 - 2 * (s % 2)) for s in range(shots)]
    both = own + lax.ppermute(other, "shot", pair)
    groups = [[2 * k + c for k in range(blocks)] for c in range(2)]
    parts = lax.all_to_all(both, "shot", 0, 0, tiled=True, axis_index_groups=groups)
    return jnp.sum(parts, axis=0).reshape(1, depth, span, size)


def solution(mesh):
    field = P("shot", "dom", None, None)
    placed = (field,) * 5 + (P("shot", None, None, None), P("shot"), P("shot"))
    return jax.shard_map(shards, mesh=mesh, in_specs=placed, out_specs=field, check_vma=False)
```

```python
import functools

import jax
import jax.numpy as jnp
from jax import lax
from jax.experimental import pallas as pl
from jax.experimental.pallas import tpu as pltpu
from jax.sharding import PartitionSpec as P


class Lateral:
    def __init__(self, width, size):
        row = lax.broadcasted_iota(jnp.int32, (width, size), 0)
        column = lax.broadcasted_iota(jnp.int32, (width, size), 1)
        self.width, self.size = width, size
        self.top, self.bottom = row == 0, row == width - 1
        self.first, self.last = column == 0, column == size - 1

    def __call__(self, middle):
        above = jnp.where(self.top, 0.0, pltpu.roll(middle, 1, 0))
        below = jnp.where(self.bottom, 0.0, pltpu.roll(middle, self.width - 1, 0))
        left = jnp.where(self.first, 0.0, pltpu.roll(middle, 1, 1))
        right = jnp.where(self.last, 0.0, pltpu.roll(middle, self.size - 1, 1))
        return (above + below) + (left + right) - 6.0 * middle


def edges(steps, depth, vel, wave, wave_old, adj, adj_old, up, down, *scratch):
    _, _, width, size = vel.shape
    lateral = Lateral(width, size)
    fetched, sems = scratch[:5], scratch[5]
    copies = [
        [
            pltpu.make_async_copy(ref.at[0, pl.ds(begin, steps)], held.at[side], sems.at[side, i])
            for i, (ref, held) in enumerate(zip((vel, wave, wave_old, adj, adj_old), fetched))
        ]
        for side, begin in enumerate((0, depth - steps))
    ]
    for copy in copies[0] + copies[1]:
        copy.start()
    vel, wave, wave_old, adj, adj_old = fetched
    for out, top in ((down, False), (up, True)):
        side = int(top)
        for copy in copies[side]:
            copy.wait()
        at = [steps - 1 - k if top else k for k in range(steps)]
        v = [vel[side, z] for z in at]
        out[2 * steps] = v[0]
        out[2 * steps + 1] = v[1]
        now, old = [wave[side, z] for z in at], [wave_old[side, z] for z in at[:-1]]
        out[0] = now[0]
        for step in range(1, steps):
            new = []
            for k in range(steps - step):
                lap = lateral(now[k]) + now[k + 1]
                if k > 0:
                    lap = lap + now[k - 1]
                new.append(2.0 * now[k] - old[k] + v[k] * lap)
            now, old = new, now
            out[step] = now[0]
        now, old = [adj[side, z] for z in at], [adj_old[side, z] for z in at[:-1]]
        scaled = [c * q for c, q in zip(v, now)]
        out[steps] = scaled[0]
        for step in range(1, steps):
            new = []
            for k in range(steps - step):
                lap = lateral(scaled[k]) + scaled[k + 1]
                if k > 0:
                    lap = lap + scaled[k - 1]
                new.append(2.0 * now[k] - old[k] + lap)
            now, old = new, now
            scaled = [c * q for c, q in zip(v, now)]
            out[steps + step] = scaled[0]


def slab(steps, depth, *refs):
    vel, wave, wave_old, adj, adj_old, residuals = [ref.at[0] for ref in refs[:6]]
    refs = refs[6:]
    laps, adjoints, img = refs[:steps], refs[steps : 2 * steps], refs[2 * steps]
    refs = refs[2 * steps + 1 :]
    ps, ws = refs[:2], refs[2:]
    _, width, size = vel.shape
    lateral = Lateral(width, size)
    blank = jnp.zeros((width, size), jnp.float32)
    for ref in (*ps, *ws):
        ref[0] = blank
        ref[depth + 1] = blank

    for z in range(depth):
        ps[0][z + 1] = wave[z]
        ws[0][z + 1] = vel[z] * adj[z]

    surface = jnp.where(lax.axis_index("dom") == 0, 1.0, 0.0)
    fields = (adj_old, adj, *adjoints)
    for step in range(steps):
        source, target = ws[step % 2], ws[(step + 1) % 2]
        old, now, new = fields[step : step + 3]
        for z in range(depth):
            lap = lateral(source[z + 1]) + (source[z] + source[z + 2])
            q = 2.0 * now[z] - old[z] + lap
            if z == 0:
                q = q + surface * residuals[step]
            new[z] = q
            if step < steps - 1:
                target[z + 1] = vel[z] * q

    for step in range(steps):
        source, target = ps[step % 2], ps[(step + 1) % 2]
        for z in range(depth):
            middle = source[z + 1]
            lap = lateral(middle) + (source[z] + source[z + 2])
            term = lap * adjoints[steps - 1 - step][z]
            if step > 0:
                term = term + img[z]
            laps[step][z] = lap
            img[z] = term
            if step < steps - 1:
                old = wave_old[z] if step == 0 else target[z + 1]
                target[z + 1] = 2.0 * middle - old + vel[z] * lap


def snake(k):
    return k ^ (k // 2 % 2) if isinstance(k, int) else k + lax.rem(lax.div(k, 2), 2) * (1 - 2 * lax.rem(k, 2))


def finish(steps, depth, blocks, *refs):
    offset, count, vel, up, down, low, high = refs[:7]
    vel = vel.at[0]
    laps, adjoints, img = refs[7 : 7 + steps], refs[7 + steps : 7 + 2 * steps], refs[7 + 2 * steps]
    own, other, blocked = refs[8 + 2 * steps :]
    _, width, size = vel.shape
    lateral = Lateral(width, size)
    span = width // blocks

    def store(z, plane):
        for j in range(blocks):
            blocked[j, z * span : (z + 1) * span, :] = plane[j * span : (j + 1) * span, :]

    for z in range(steps, depth - steps):
        store(z, img[z])

    for sent, got, top in ((down, low, False), (up, high, True)):
        at = [depth - 1 - k if top else k for k in range(steps)]
        here = [vel[z] for z in at]
        there = [got[2 * steps], got[2 * steps + 1]]

        def march(first, scale_field):
            f = [sent[first + n] for n in range(steps)]
            g = [got[first + n] for n in range(steps)]
            corrections, fields = [], []
            h_now, h_old, t_now, t_old = [], [], [], []
            for step in range(steps):
                if scale_field:
                    hs = [c * x for c, x in zip(here, h_now)]
                    ts = [c * x for c, x in zip(there, t_now)]
                else:
                    hs, ts = h_now, t_now
                laps_here = []
                for k in range(step + 1):
                    lap = g[step] if k == 0 else hs[k - 1]
                    if k == 0 and step > 0:
                        lap = lap + ts[0]
                    if k < len(hs):
                        lap = lap + lateral(hs[k])
                    if k + 1 < len(hs):
                        lap = lap + hs[k + 1]
                    laps_here.append(lap)
                corrections.append(laps_here)
                last = step == steps - 1
                new_h, new_t = [], []
                if scale_field or not last:
                    for k, lap in enumerate(laps_here):
                        x = lap if scale_field else here[k] * lap
                        if k < len(h_now):
                            x = x + 2.0 * h_now[k]
                        if k < len(h_old):
                            x = x - h_old[k]
                        new_h.append(x)
                if not last:
                    for k in range(min(step + 1, steps - 1 - step)):
                        lap = f[step] if k == 0 else ts[k - 1]
                        if k == 0 and step > 0:
                            lap = lap + hs[0]
                        if k < len(ts):
                            lap = lap + lateral(ts[k])
                        if k + 1 < len(ts):
                            lap = lap + ts[k + 1]
                        x = lap if scale_field else there[k] * lap
                        if k < len(t_now):
                            x = x + 2.0 * t_now[k]
                        if k < len(t_old):
                            x = x - t_old[k]
                        new_t.append(x)
                fields.append(new_h)
                h_now, h_old, t_now, t_old = new_h, h_now, new_t, t_now
            return corrections, fields

        more_laps, _ = march(0, False)
        _, more_adjoints = march(steps, True)
        for k, z in enumerate(at):
            total = None
            for n in range(steps):
                a = laps[n][z]
                if k < len(more_laps[n]):
                    a = a + more_laps[n][k]
                b = adjoints[steps - 1 - n][z]
                if k < len(more_adjoints[steps - 1 - n]):
                    b = b + more_adjoints[steps - 1 - n][k]
                total = a * b if total is None else total + a * b
            store(z, total)

    start, live = offset[0], count[0]
    odd = lax.rem(start + lax.axis_index("shot"), 2)
    zero = jnp.zeros((depth * span, size), jnp.float32)
    half = blocks // 2

    @pl.loop(0, half)
    def _(i):
        for ref, j in ((own, 2 * i + odd), (other, 2 * i + 1 - odd)):
            k = snake(lax.div(start + j, 2))
            ref[k] = jnp.where(j < live, blocked[j], 0.0)
            ref[lax.rem(k + half, blocks)] = zero


def shards(vel, wave, wave_old, adj, adj_old, residuals, offset, count):
    _, depth, width, size = vel.shape
    steps = residuals.shape[1]
    shots, doms = lax.axis_size("shot"), lax.axis_size("dom")
    blocks = shots // 2
    span = width // blocks
    f32 = jnp.float32
    hbm = pl.BlockSpec(memory_space=pltpu.HBM)
    smem = pl.BlockSpec(memory_space=pltpu.SMEM)
    vmem = pl.BlockSpec(memory_space=pltpu.VMEM)
    room = pltpu.CompilerParams(vmem_limit_bytes=24 * 2**20)
    message = jax.ShapeDtypeStruct((2 * steps + 2, width, size), f32)
    field = jax.ShapeDtypeStruct((depth, width, size), f32)
    block = jax.ShapeDtypeStruct((blocks, depth * span, size), f32)

    up, down = pl.pallas_call(
        functools.partial(edges, steps, depth),
        out_shape=(message, message),
        in_specs=[hbm] * 5,
        out_specs=(vmem, vmem),
        scratch_shapes=[pltpu.VMEM((2, steps, width, size), f32)] * 5 + [pltpu.SemaphoreType.DMA((2, 5))],
        compiler_params=pltpu.CompilerParams(vmem_limit_bytes=53 * 2**20),
    )(vel, wave, wave_old, adj, adj_old)

    low = lax.ppermute(up, "dom", [(i, i + 1) for i in range(doms - 1)])
    high = lax.ppermute(down, "dom", [(i + 1, i) for i in range(doms - 1)])

    inner = pl.pallas_call(
        functools.partial(slab, steps, depth),
        out_shape=(field,) * (2 * steps + 1),
        in_specs=[vmem] * 6,
        out_specs=(vmem,) * (2 * steps + 1),
        scratch_shapes=[pltpu.VMEM((depth + 2, width, size), f32)] * 4,
        cost_estimate=pl.CostEstimate(flops=40_000_000, bytes_accessed=16_000_000, transcendentals=0),
        compiler_params=room,
    )(vel, wave, wave_old, adj, adj_old, residuals)

    own, other = pl.pallas_call(
        functools.partial(finish, steps, depth, blocks),
        out_shape=(block, block),
        in_specs=[smem, smem] + [vmem] * (6 + 2 * steps),
        out_specs=(vmem, vmem),
        scratch_shapes=[pltpu.VMEM((blocks, depth * span, size), f32)],
        compiler_params=room,
    )(offset, count, vel, up, down, low, high, *inner)

    pair = [(s, s + 1 - 2 * (s % 2)) for s in range(shots)]
    both = own + lax.ppermute(other, "shot", pair)
    groups = [[2 * snake(k) + c for k in range(blocks)] for c in range(2)]
    parts = lax.all_to_all(both, "shot", 0, 0, tiled=True, axis_index_groups=groups)
    return jnp.sum(parts, axis=0).reshape(1, depth, span, size)


def solution(mesh):
    field = P("shot", "dom", None, None)
    placed = (field,) * 5 + (P("shot", None, None, None), P("shot"), P("shot"))
    return jax.shard_map(shards, mesh=mesh, in_specs=placed, out_specs=field, check_vma=False)
```

```python
import functools

import jax
import jax.numpy as jnp
from jax import lax
from jax.experimental import pallas as pl
from jax.experimental.pallas import tpu as pltpu
from jax.sharding import PartitionSpec as P


class Lateral:
    def __init__(self, width, size):
        row = lax.broadcasted_iota(jnp.int32, (width, size), 0)
        column = lax.broadcasted_iota(jnp.int32, (width, size), 1)
        self.width, self.size = width, size
        self.top, self.bottom = row == 0, row == width - 1
        self.first, self.last = column == 0, column == size - 1

    def __call__(self, middle):
        above = jnp.where(self.top, 0.0, pltpu.roll(middle, 1, 0))
        below = jnp.where(self.bottom, 0.0, pltpu.roll(middle, self.width - 1, 0))
        left = jnp.where(self.first, 0.0, pltpu.roll(middle, 1, 1))
        right = jnp.where(self.last, 0.0, pltpu.roll(middle, self.size - 1, 1))
        return (above + below) + (left + right) - 6.0 * middle


def edges(steps, depth, vel, wave, wave_old, adj, adj_old, down, up, *scratch):
    _, _, width, size = vel.shape
    lateral = Lateral(width, size)
    fetched, sems = scratch[:5], scratch[5]
    copies = [
        [
            pltpu.make_async_copy(ref.at[0, pl.ds(begin, steps)], held.at[side], sems.at[side, i])
            for i, (ref, held) in enumerate(zip((vel, wave, wave_old, adj, adj_old), fetched))
        ]
        for side, begin in enumerate((0, depth - steps))
    ]
    for copy in copies[0] + copies[1]:
        copy.start()
    vel, wave, wave_old, adj, adj_old = fetched
    for out, top in ((down, False), (up, True)):
        side = int(top)
        for copy in copies[side]:
            copy.wait()
        at = [steps - 1 - k if top else k for k in range(steps)]
        v = [vel[side, z] for z in at]
        out[2 * steps] = v[0]
        out[2 * steps + 1] = v[1]
        now, old = [wave[side, z] for z in at], [wave_old[side, z] for z in at[:-1]]
        out[0] = now[0]
        for step in range(1, steps):
            new = []
            for k in range(steps - step):
                lap = lateral(now[k]) + now[k + 1]
                if k > 0:
                    lap = lap + now[k - 1]
                new.append(2.0 * now[k] - old[k] + v[k] * lap)
            now, old = new, now
            out[step] = now[0]
        now, old = [adj[side, z] for z in at], [adj_old[side, z] for z in at[:-1]]
        scaled = [c * q for c, q in zip(v, now)]
        out[steps] = scaled[0]
        for step in range(1, steps):
            new = []
            for k in range(steps - step):
                lap = lateral(scaled[k]) + scaled[k + 1]
                if k > 0:
                    lap = lap + scaled[k - 1]
                new.append(2.0 * now[k] - old[k] + lap)
            now, old = new, now
            scaled = [c * q for c, q in zip(v, now)]
            out[steps + step] = scaled[0]


def slab(steps, depth, *refs):
    vel, wave, wave_old, adj, adj_old, residuals = [ref.at[0] for ref in refs[:6]]
    refs = refs[6:]
    laps, adjoints, img = refs[:steps], refs[steps : 2 * steps], refs[2 * steps]
    refs = refs[2 * steps + 1 :]
    ps, ws = refs[:2], refs[2:]
    _, width, size = vel.shape
    lateral = Lateral(width, size)
    blank = jnp.zeros((width, size), jnp.float32)
    for ref in (*ps, *ws):
        ref[0] = blank
        ref[depth + 1] = blank

    for z in range(depth):
        ps[0][z + 1] = wave[z]
        ws[0][z + 1] = vel[z] * adj[z]

    surface = jnp.where(lax.axis_index("dom") == 0, 1.0, 0.0)
    fields = (adj_old, adj, *adjoints)
    for step in range(steps):
        source, target = ws[step % 2], ws[(step + 1) % 2]
        old, now, new = fields[step : step + 3]
        for z in range(depth):
            lap = lateral(source[z + 1]) + (source[z] + source[z + 2])
            q = 2.0 * now[z] - old[z] + lap
            if z == 0:
                q = q + surface * residuals[step]
            new[z] = q
            if step < steps - 1:
                target[z + 1] = vel[z] * q

    for step in range(steps):
        source, target = ps[step % 2], ps[(step + 1) % 2]
        for z in range(depth):
            middle = source[z + 1]
            lap = lateral(middle) + (source[z] + source[z + 2])
            term = lap * adjoints[steps - 1 - step][z]
            if step > 0:
                term = term + img[z]
            laps[step][z] = lap
            img[z] = term
            if step < steps - 1:
                old = wave_old[z] if step == 0 else target[z + 1]
                target[z + 1] = 2.0 * middle - old + vel[z] * lap


def snake(k):
    return k ^ (k // 2 % 2) if isinstance(k, int) else k + lax.rem(lax.div(k, 2), 2) * (1 - 2 * lax.rem(k, 2))


def finish(steps, depth, blocks, *refs):
    offset, count, vel, down, up, high, low = refs[:7]
    vel = vel.at[0]
    laps, adjoints, img = refs[7 : 7 + steps], refs[7 + steps : 7 + 2 * steps], refs[7 + 2 * steps]
    own, other, blocked = refs[8 + 2 * steps :]
    _, width, size = vel.shape
    lateral = Lateral(width, size)
    span = width // blocks

    def store(z, plane):
        for j in range(blocks):
            blocked[j, z * span : (z + 1) * span, :] = plane[j * span : (j + 1) * span, :]

    for z in range(steps, depth - steps):
        store(z, img[z])

    for sent, got, top in ((down, low, False), (up, high, True)):
        at = [depth - 1 - k if top else k for k in range(steps)]
        here = [vel[z] for z in at]
        there = [got[2 * steps], got[2 * steps + 1]]

        def march(first, scale_field):
            f = [sent[first + n] for n in range(steps)]
            g = [got[first + n] for n in range(steps)]
            corrections, fields = [], []
            h_now, h_old, t_now, t_old = [], [], [], []
            for step in range(steps):
                if scale_field:
                    hs = [c * x for c, x in zip(here, h_now)]
                    ts = [c * x for c, x in zip(there, t_now)]
                else:
                    hs, ts = h_now, t_now
                laps_here = []
                for k in range(step + 1):
                    lap = g[step] if k == 0 else hs[k - 1]
                    if k == 0 and step > 0:
                        lap = lap + ts[0]
                    if k < len(hs):
                        lap = lap + lateral(hs[k])
                    if k + 1 < len(hs):
                        lap = lap + hs[k + 1]
                    laps_here.append(lap)
                corrections.append(laps_here)
                last = step == steps - 1
                new_h, new_t = [], []
                if scale_field or not last:
                    for k, lap in enumerate(laps_here):
                        x = lap if scale_field else here[k] * lap
                        if k < len(h_now):
                            x = x + 2.0 * h_now[k]
                        if k < len(h_old):
                            x = x - h_old[k]
                        new_h.append(x)
                if not last:
                    for k in range(min(step + 1, steps - 1 - step)):
                        lap = f[step] if k == 0 else ts[k - 1]
                        if k == 0 and step > 0:
                            lap = lap + hs[0]
                        if k < len(ts):
                            lap = lap + lateral(ts[k])
                        if k + 1 < len(ts):
                            lap = lap + ts[k + 1]
                        x = lap if scale_field else there[k] * lap
                        if k < len(t_now):
                            x = x + 2.0 * t_now[k]
                        if k < len(t_old):
                            x = x - t_old[k]
                        new_t.append(x)
                fields.append(new_h)
                h_now, h_old, t_now, t_old = new_h, h_now, new_t, t_now
            return corrections, fields

        more_laps, _ = march(0, False)
        _, more_adjoints = march(steps, True)
        for k, z in enumerate(at):
            total = None
            for n in range(steps):
                a = laps[n][z]
                if k < len(more_laps[n]):
                    a = a + more_laps[n][k]
                b = adjoints[steps - 1 - n][z]
                if k < len(more_adjoints[steps - 1 - n]):
                    b = b + more_adjoints[steps - 1 - n][k]
                total = a * b if total is None else total + a * b
            store(z, total)

    start, live = offset[0], count[0]
    odd = lax.rem(start + lax.axis_index("shot"), 2)
    zero = jnp.zeros((depth * span, size), jnp.float32)
    half = blocks // 2

    @pl.loop(0, half)
    def _(i):
        for ref, j in ((own, 2 * i + odd), (other, 2 * i + 1 - odd)):
            k = snake(lax.div(start + j, 2))
            ref[k] = jnp.where(j < live, blocked[j], 0.0)
            ref[lax.rem(k + half, blocks)] = zero


def shards(vel, wave, wave_old, adj, adj_old, residuals, offset, count):
    _, depth, width, size = vel.shape
    steps = residuals.shape[1]
    shots, doms = lax.axis_size("shot"), lax.axis_size("dom")
    blocks = shots // 2
    span = width // blocks
    f32 = jnp.float32
    hbm = pl.BlockSpec(memory_space=pltpu.HBM)
    smem = pl.BlockSpec(memory_space=pltpu.SMEM)
    vmem = pl.BlockSpec(memory_space=pltpu.VMEM)
    room = pltpu.CompilerParams(vmem_limit_bytes=24 * 2**20)
    message = jax.ShapeDtypeStruct((2 * steps + 2, width, size), f32)
    field = jax.ShapeDtypeStruct((depth, width, size), f32)
    block = jax.ShapeDtypeStruct((blocks, depth * span, size), f32)

    down, up = pl.pallas_call(
        functools.partial(edges, steps, depth),
        out_shape=(message, message),
        in_specs=[hbm] * 5,
        out_specs=(vmem, vmem),
        scratch_shapes=[pltpu.VMEM((2, steps, width, size), f32)] * 5 + [pltpu.SemaphoreType.DMA((2, 5))],
        compiler_params=pltpu.CompilerParams(vmem_limit_bytes=53 * 2**20),
    )(vel, wave, wave_old, adj, adj_old)

    high = lax.ppermute(down, "dom", [(i + 1, i) for i in range(doms - 1)])
    low = lax.ppermute(up, "dom", [(i, i + 1) for i in range(doms - 1)])

    inner = pl.pallas_call(
        functools.partial(slab, steps, depth),
        out_shape=(field,) * (2 * steps + 1),
        in_specs=[vmem] * 6,
        out_specs=(vmem,) * (2 * steps + 1),
        scratch_shapes=[pltpu.VMEM((depth + 2, width, size), f32)] * 4,
        cost_estimate=pl.CostEstimate(flops=40_000_000, bytes_accessed=16_000_000, transcendentals=0),
        compiler_params=room,
    )(vel, wave, wave_old, adj, adj_old, residuals)

    own, other = pl.pallas_call(
        functools.partial(finish, steps, depth, blocks),
        out_shape=(block, block),
        in_specs=[smem, smem] + [vmem] * (6 + 2 * steps),
        out_specs=(vmem, vmem),
        scratch_shapes=[pltpu.VMEM((blocks, depth * span, size), f32)],
        compiler_params=room,
    )(offset, count, vel, down, up, high, low, *inner)

    pair = [(s, s + 1 - 2 * (s % 2)) for s in range(shots)]
    both = own + lax.ppermute(other, "shot", pair)
    groups = [[2 * snake(k) + c for k in range(blocks)] for c in range(2)]
    parts = lax.all_to_all(both, "shot", 0, 0, tiled=True, axis_index_groups=groups)
    return jnp.sum(parts, axis=0).reshape(1, depth, span, size)


def solution(mesh):
    field = P("shot", "dom", None, None)
    placed = (field,) * 5 + (P("shot", None, None, None), P("shot"), P("shot"))
    return jax.shard_map(shards, mesh=mesh, in_specs=placed, out_specs=field, check_vma=False)
```

```python
import functools

import jax
import jax.numpy as jnp
from jax import lax
from jax.experimental import pallas as pl
from jax.experimental.pallas import tpu as pltpu
from jax.sharding import PartitionSpec as P


class Lateral:
    def __init__(self, width, size):
        row = lax.broadcasted_iota(jnp.int32, (width, size), 0)
        column = lax.broadcasted_iota(jnp.int32, (width, size), 1)
        self.width, self.size = width, size
        self.top, self.bottom = row == 0, row == width - 1
        self.first, self.last = column == 0, column == size - 1

    def __call__(self, middle):
        above = jnp.where(self.top, 0.0, pltpu.roll(middle, 1, 0))
        below = jnp.where(self.bottom, 0.0, pltpu.roll(middle, self.width - 1, 0))
        left = jnp.where(self.first, 0.0, pltpu.roll(middle, 1, 1))
        right = jnp.where(self.last, 0.0, pltpu.roll(middle, self.size - 1, 1))
        return (above + below) + (left + right) - 6.0 * middle


def edges(steps, depth, vel, wave, wave_old, adj, adj_old, up, down, *scratch):
    _, _, width, size = vel.shape
    lateral = Lateral(width, size)
    fetched, sems = scratch[:5], scratch[5]
    copies = [
        [
            pltpu.make_async_copy(ref.at[0, pl.ds(begin, steps)], held.at[side], sems.at[side, i])
            for i, (ref, held) in enumerate(zip((vel, wave, wave_old, adj, adj_old), fetched))
        ]
        for side, begin in enumerate((0, depth - steps))
    ]
    for copy in copies[0] + copies[1]:
        copy.start()
    vel, wave, wave_old, adj, adj_old = fetched
    for out, top in ((down, False), (up, True)):
        side = int(top)
        for copy in copies[side]:
            copy.wait()
        at = [steps - 1 - k if top else k for k in range(steps)]
        v = [vel[side, z] for z in at]
        out[2 * steps] = v[0]
        out[2 * steps + 1] = v[1]
        now, old = [wave[side, z] for z in at], [wave_old[side, z] for z in at[:-1]]
        out[0] = now[0]
        for step in range(1, steps):
            new = []
            for k in range(steps - step):
                lap = lateral(now[k]) + now[k + 1]
                if k > 0:
                    lap = lap + now[k - 1]
                new.append(2.0 * now[k] - old[k] + v[k] * lap)
            now, old = new, now
            out[step] = now[0]
        now, old = [adj[side, z] for z in at], [adj_old[side, z] for z in at[:-1]]
        scaled = [c * q for c, q in zip(v, now)]
        out[steps] = scaled[0]
        for step in range(1, steps):
            new = []
            for k in range(steps - step):
                lap = lateral(scaled[k]) + scaled[k + 1]
                if k > 0:
                    lap = lap + scaled[k - 1]
                new.append(2.0 * now[k] - old[k] + lap)
            now, old = new, now
            scaled = [c * q for c, q in zip(v, now)]
            out[steps + step] = scaled[0]


def slab(steps, depth, *refs):
    vel, wave, wave_old, adj, adj_old, residuals = [ref.at[0] for ref in refs[:6]]
    refs = refs[6:]
    laps, adjoints, img = refs[:steps], refs[steps : 2 * steps], refs[2 * steps]
    refs = refs[2 * steps + 1 :]
    ps, ws = refs[:2], refs[2:]
    _, width, size = vel.shape
    lateral = Lateral(width, size)
    blank = jnp.zeros((width, size), jnp.float32)
    for ref in (*ps, *ws):
        ref[0] = blank
        ref[depth + 1] = blank

    for z in range(depth):
        ps[0][z + 1] = wave[z]
        ws[0][z + 1] = vel[z] * adj[z]

    surface = jnp.where(lax.axis_index("dom") == 0, 1.0, 0.0)
    fields = (adj_old, adj, *adjoints)
    for step in range(steps):
        source, target = ws[step % 2], ws[(step + 1) % 2]
        old, now, new = fields[step : step + 3]
        for z in range(depth):
            lap = lateral(source[z + 1]) + (source[z] + source[z + 2])
            q = 2.0 * now[z] - old[z] + lap
            if z == 0:
                q = q + surface * residuals[step]
            new[z] = q
            if step < steps - 1:
                target[z + 1] = vel[z] * q

    for step in range(steps):
        source, target = ps[step % 2], ps[(step + 1) % 2]
        for z in range(depth):
            middle = source[z + 1]
            lap = lateral(middle) + (source[z] + source[z + 2])
            term = lap * adjoints[steps - 1 - step][z]
            if step > 0:
                term = term + img[z]
            laps[step][z] = lap
            img[z] = term
            if step < steps - 1:
                old = wave_old[z] if step == 0 else target[z + 1]
                target[z + 1] = 2.0 * middle - old + vel[z] * lap


def finish(steps, depth, blocks, *refs):
    offset, count, vel, up, down, low, high = refs[:7]
    vel = vel.at[0]
    laps, adjoints, img = refs[7 : 7 + steps], refs[7 + steps : 7 + 2 * steps], refs[7 + 2 * steps]
    own, other, blocked = refs[8 + 2 * steps :]
    _, width, size = vel.shape
    lateral = Lateral(width, size)
    span = width // blocks

    def store(z, plane):
        for j in range(blocks):
            blocked[j, z * span : (z + 1) * span, :] = plane[j * span : (j + 1) * span, :]

    for z in range(steps, depth - steps):
        store(z, img[z])

    for sent, got, top in ((down, low, False), (up, high, True)):
        at = [depth - 1 - k if top else k for k in range(steps)]
        here = [vel[z] for z in at]
        there = [got[2 * steps], got[2 * steps + 1]]

        def march(first, scale_field):
            f = [sent[first + n] for n in range(steps)]
            g = [got[first + n] for n in range(steps)]
            corrections, fields = [], []
            h_now, h_old, t_now, t_old = [], [], [], []
            for step in range(steps):
                if scale_field:
                    hs = [c * x for c, x in zip(here, h_now)]
                    ts = [c * x for c, x in zip(there, t_now)]
                else:
                    hs, ts = h_now, t_now
                laps_here = []
                for k in range(step + 1):
                    lap = g[step] if k == 0 else hs[k - 1]
                    if k == 0 and step > 0:
                        lap = lap + ts[0]
                    if k < len(hs):
                        lap = lap + lateral(hs[k])
                    if k + 1 < len(hs):
                        lap = lap + hs[k + 1]
                    laps_here.append(lap)
                corrections.append(laps_here)
                last = step == steps - 1
                new_h, new_t = [], []
                if scale_field or not last:
                    for k, lap in enumerate(laps_here):
                        x = lap if scale_field else here[k] * lap
                        if k < len(h_now):
                            x = x + 2.0 * h_now[k]
                        if k < len(h_old):
                            x = x - h_old[k]
                        new_h.append(x)
                if not last:
                    for k in range(min(step + 1, steps - 1 - step)):
                        lap = f[step] if k == 0 else ts[k - 1]
                        if k == 0 and step > 0:
                            lap = lap + hs[0]
                        if k < len(ts):
                            lap = lap + lateral(ts[k])
                        if k + 1 < len(ts):
                            lap = lap + ts[k + 1]
                        x = lap if scale_field else there[k] * lap
                        if k < len(t_now):
                            x = x + 2.0 * t_now[k]
                        if k < len(t_old):
                            x = x - t_old[k]
                        new_t.append(x)
                fields.append(new_h)
                h_now, h_old, t_now, t_old = new_h, h_now, new_t, t_now
            return corrections, fields

        more_laps, _ = march(0, False)
        _, more_adjoints = march(steps, True)
        for k, z in enumerate(at):
            total = None
            for n in range(steps):
                a = laps[n][z]
                if k < len(more_laps[n]):
                    a = a + more_laps[n][k]
                b = adjoints[steps - 1 - n][z]
                if k < len(more_adjoints[steps - 1 - n]):
                    b = b + more_adjoints[steps - 1 - n][k]
                total = a * b if total is None else total + a * b
            store(z, total)

    start, live = offset[0], count[0]
    odd = lax.rem(start + lax.axis_index("shot"), 2)
    zero = jnp.zeros((depth * span, size), jnp.float32)
    half = blocks // 2

    @pl.loop(0, half)
    def _(i):
        for ref, j in ((own, 2 * i + odd), (other, 2 * i + 1 - odd)):
            k = lax.div(start + j, 2)
            ref[k] = jnp.where(j < live, blocked[j], 0.0)
            ref[lax.rem(k + half, blocks)] = zero


def shards(vel, wave, wave_old, adj, adj_old, residuals, offset, count):
    _, depth, width, size = vel.shape
    steps = residuals.shape[1]
    shots, doms = lax.axis_size("shot"), lax.axis_size("dom")
    blocks = shots // 2
    span = width // blocks
    f32 = jnp.float32
    hbm = pl.BlockSpec(memory_space=pltpu.HBM)
    smem = pl.BlockSpec(memory_space=pltpu.SMEM)
    vmem = pl.BlockSpec(memory_space=pltpu.VMEM)
    room = pltpu.CompilerParams(vmem_limit_bytes=24 * 2**20)
    message = jax.ShapeDtypeStruct((2 * steps + 2, width, size), f32)
    field = jax.ShapeDtypeStruct((depth, width, size), f32)
    block = jax.ShapeDtypeStruct((blocks, depth * span, size), f32)

    up, down = pl.pallas_call(
        functools.partial(edges, steps, depth),
        out_shape=(message, message),
        in_specs=[hbm] * 5,
        out_specs=(vmem, vmem),
        scratch_shapes=[pltpu.VMEM((2, steps, width, size), f32)] * 5 + [pltpu.SemaphoreType.DMA((2, 5))],
        compiler_params=pltpu.CompilerParams(vmem_limit_bytes=53 * 2**20),
    )(vel, wave, wave_old, adj, adj_old)

    low = lax.ppermute(up, "dom", [(i, i + 1) for i in range(doms - 1)])
    high = lax.ppermute(down, "dom", [(i + 1, i) for i in range(doms - 1)])

    inner = pl.pallas_call(
        functools.partial(slab, steps, depth),
        out_shape=(field,) * (2 * steps + 1),
        in_specs=[vmem] * 6,
        out_specs=(vmem,) * (2 * steps + 1),
        scratch_shapes=[pltpu.VMEM((depth + 2, width, size), f32)] * 4,
        cost_estimate=pl.CostEstimate(flops=40_000_000, bytes_accessed=16_000_000, transcendentals=0),
        compiler_params=room,
    )(vel, wave, wave_old, adj, adj_old, residuals)

    own, other = pl.pallas_call(
        functools.partial(finish, steps, depth, blocks),
        out_shape=(block, block),
        in_specs=[smem, smem] + [vmem] * (6 + 2 * steps),
        out_specs=(vmem, vmem),
        scratch_shapes=[pltpu.VMEM((blocks, depth * span, size), f32)],
        compiler_params=room,
    )(offset, count, vel, up, down, low, high, *inner)

    pair = [(s, s + 1 - 2 * (s % 2)) for s in range(shots)]
    both = own + lax.ppermute(other, "shot", pair)
    groups = [[2 * k + c for k in range(blocks)] for c in range(2)]
    parts = lax.all_to_all(both, "shot", 0, 0, tiled=True, axis_index_groups=groups)
    return jnp.sum(parts, axis=0).reshape(1, depth, span, size)


def solution(mesh):
    field = P("shot", "dom", None, None)
    placed = (field,) * 5 + (P("shot", None, None, None), P("shot"), P("shot"))
    return jax.shard_map(shards, mesh=mesh, in_specs=placed, out_specs=field, check_vma=False)
```
